32 devices in a mesh: plane: 2 (over x), span: 4 (over z), height: 4 (over y, core).
Axes of the slice: x: 2, y: 2, z: 4, core: 2. Of those that a mesh axis runs over, the one named last changes fastest.
Arguments:
- noisy: bfloat16 [2, 3, 256, 512], P('plane', None, 'height', 'span'), may hold values from -6 to 6
- coarse_cond: bfloat16 [32, 2, 3, 32, 64], P(('plane', 'span', 'height')), may hold values from -6 to 6
- timestep: int32 [1], replicated, may hold values from 20 to 899
- owner: int32 [1], replicated, may hold values from 0 to 31
- w_embed: float32 [64, 256], replicated, may hold values from -0.75 to 0.75
- w_biases: float32 [256, 448], replicated, may hold values from -0.375 to 0.375
- w_enter: bfloat16 [3, 64, 18], replicated, may hold values from -1.5 to 1.5
- pool_fine: bfloat16 [4, 128, 64], replicated, may hold values from -0.5 to 0.5
- pool_mid: bfloat16 [4, 256, 128], replicated, may hold values from -0.375 to 0.375
- w_squeeze: bfloat16 [128, 256], replicated, may hold values from -0.375 to 0.375
- w_across: bfloat16 [3, 256, 128], replicated, may hold values from -0.5 to 0.5
- w_middle: bfloat16 [3, 256, 768], replicated, may hold values from -0.21875 to 0.21875
- rise_mid: bfloat16 [4, 128, 256], replicated, may hold values from -0.5 to 0.5
- decode_mid: bfloat16 [3, 128, 384], replicated, may hold values from -0.3125 to 0.3125
- rise_fine: bfloat16 [4, 64, 128], replicated, may hold values from -0.75 to 0.75
- decode_fine: bfloat16 [3, 64, 192], replicated, may hold values from -0.4375 to 0.4375
- w_leave: bfloat16 [3, 3, 192], replicated, may hold values from -0.4375 to 0.4375
Outputs:
- noise_pred: bfloat16 [2, 3, 256, 512], P('plane', None, 'height', 'span')
- next_sample: float32 [2, 3, 256, 512], P('plane', None, 'height', 'span')
The draws below stay inside these ranges and needn't reach their ends.
Inputs may be any that keep to these rules, and one draw needn't show every extreme that they name: The timestep lies in the plan's range and is at least 20. The owner is a device index in the mesh order plane, span, height.
All inputs are finite; a program needn't handle non-finite values.
Results may differ from the reference program's by a relative error of at most 0.03.
Values may be sent and summed in bfloat16 or wider, within the bound.
No kernel may reach another device: no remote copies, remote signals or barrier semaphores. Data moves between devices by JAX's collectives and lax.ppermute only.
A program may use at most 64 MiB of HBM per device.

```python
import math
import jax
import jax.numpy as jnp
from jax import lax

CH1 = 64
CH2 = 128
CH3 = 256
INNER = 128
TSIN = 64
TEMB = 256
CF = 8
TSTEPS = 1000
STRIDE = 20
NP = 2
HEIGHT = 256
SPAN = 512
CHC = 32
CSC = 64
DEVICES = 32


def level_of(rng, shape, split, smallest, high):
    def one(dim, parts):
        heights = jax.random.uniform(jax.random.fold_in(jax.random.fold_in(rng, 6), dim), (parts,), jnp.float32, smallest / len(split), high / len(split))
        return jnp.repeat(jnp.exp(heights), shape[dim] // parts).reshape((-1,) + (1,) * (len(shape) - dim - 1))

    factor_of = one(*split[0])
    for cut in split[1:]:
        factor_of = factor_of * one(*cut)
    return factor_of


def centred(own_key, extent, scale, limit, split=(), kind=jnp.bfloat16):
    entries = scale * jax.random.normal(own_key, extent, jnp.float32)
    if split:
        entries = entries * level_of(own_key, extent, split, -0.22, 0.18)
    return jnp.clip(entries, -limit, limit).astype(kind)


def setup_inputs(seed: int = 0) -> dict:
    key_list = jax.random.split(jax.random.key(seed), 18)
    noisy = centred(key_list[0], (NP, 3, HEIGHT, SPAN), 1.0, 6.0, ((0, 2), (2, 4), (3, 4)))
    coarse_cond = centred(key_list[1], (DEVICES, NP, 3, CHC, CSC), 1.0, 6.0, ((0, 32),))
    timestep = jax.random.randint(key_list[2], (1,), STRIDE, 900).astype(jnp.int32)
    owner = jax.random.randint(key_list[3], (1,), 0, DEVICES).astype(jnp.int32)
    w_embed = centred(key_list[4], (TSIN, TEMB), TSIN ** -0.5, 0.75, (), jnp.float32)
    w_biases = centred(key_list[5], (TEMB, CH1 + CH2 + CH3), TEMB ** -0.5, 0.375, (), jnp.float32)
    w_enter = centred(key_list[6], (3, CH1, 18), 18 ** -0.5, 1.5)
    pool_fine = centred(key_list[7], (4, CH2, CH1), (2 * CH1) ** -0.5, 0.5)
    pool_mid = centred(key_list[8], (4, CH3, CH2), (2 * CH2) ** -0.5, 0.375)
    w_squeeze = centred(key_list[9], (INNER, CH3), CH3 ** -0.5, 0.375)
    w_across = centred(key_list[10], (3, CH3, INNER), INNER ** -0.5, 0.5)
    w_middle = centred(key_list[11], (3, CH3, 3 * CH3), (3 * CH3) ** -0.5, 0.21875)
    rise_mid = centred(key_list[12], (4, CH2, CH3), (CH3 // 2) ** -0.5, 0.5)
    decode_mid = centred(key_list[13], (3, CH2, 3 * CH2), (3 * CH2) ** -0.5, 0.3125)
    rise_fine = centred(key_list[14], (4, CH1, CH2), (CH2 // 2) ** -0.5, 0.75)
    decode_fine = centred(key_list[15], (3, CH1, 3 * CH1), (3 * CH1) ** -0.5, 0.4375)
    w_leave = centred(key_list[16], (3, 3, 3 * CH1), (3 * CH1) ** -0.5, 0.4375)
    return {"noisy": noisy, "coarse_cond": coarse_cond, "timestep": timestep, "owner": owner, "w_embed": w_embed, "w_biases": w_biases, "w_enter": w_enter, "pool_fine": pool_fine, "pool_mid": pool_mid, "w_squeeze": w_squeeze, "w_across": w_across, "w_middle": w_middle, "rise_mid": rise_mid, "decode_mid": decode_mid, "rise_fine": rise_fine, "decode_fine": decode_fine, "w_leave": w_leave}


def stencil(padded, weight, rows, cols):
    total = None
    for lift in range(3):
        stacked = jnp.concatenate([padded[:, lift:lift + rows, step:step + cols] for step in range(3)], axis=0)
        term = jnp.einsum('ok,khs->ohs', weight[lift].astype(jnp.float32), stacked.astype(jnp.float32), precision=lax.Precision.HIGHEST)
        total = term if total is None else total + term
    return total

def framed(field):
    return jnp.pad(field, ((0, 0), (1, 1), (1, 1)))

def pooled(field, weight):
    chans, rows, cols = field.shape
    outs = weight.shape[1]
    grid = field.reshape(chans, rows // 2, 2, cols // 2, 2).astype(jnp.float32)
    kernel = weight.reshape(2, 2, outs, chans).astype(jnp.float32)
    return jnp.einsum('aboc,cxayb->oxy', kernel, grid, precision=lax.Precision.HIGHEST)

def raised(field, weight):
    chans, rows, cols = field.shape
    outs = weight.shape[1]
    kernel = weight.reshape(2, 2, outs, chans).astype(jnp.float32)
    spread = jnp.einsum('aboc,cxy->oxayb', kernel, field.astype(jnp.float32), precision=lax.Precision.HIGHEST)
    return spread.reshape(outs, 2 * rows, 2 * cols)

def plan(stepnum):
    phase = (stepnum.astype(jnp.float32) / TSTEPS + 0.008) / 1.008 * (math.pi / 2.0)
    return jnp.cos(phase) ** 2

def time_bias(timestep, w_embed, w_biases):
    half = w_embed.shape[0] // 2
    freqs = jnp.exp(-math.log(10000.0) * jnp.arange(half, dtype=jnp.float32) / half)
    angles = timestep[0].astype(jnp.float32) * freqs
    waves = jnp.concatenate([jnp.sin(angles), jnp.cos(angles)])
    hidden = jax.nn.silu(jnp.dot(waves, w_embed, precision=lax.Precision.HIGHEST))
    return jnp.dot(hidden, w_biases, precision=lax.Precision.HIGHEST)

def reference(noisy, coarse_cond, timestep, owner, w_embed, w_biases, w_enter, pool_fine, pool_mid, w_squeeze, w_across, w_middle, rise_mid, decode_mid, rise_fine, decode_fine, w_leave):
    biases = time_bias(timestep, w_embed, w_biases)
    first = w_enter.shape[1]
    second = pool_fine.shape[1]
    bias_one = biases[:first][:, None, None]
    bias_two = biases[first:first + second][:, None, None]
    bias_three = biases[first + second:][:, None, None]
    cond = lax.dynamic_index_in_dim(coarse_cond, owner[0].astype(jnp.int32), 0, keepdims=False)
    lifted = jnp.repeat(jnp.repeat(cond, CF, axis=2), CF, axis=3)

    def encode(pair):
        sample, lift = pair
        rows, cols = (sample.shape[1], sample.shape[2])
        entry = jnp.concatenate([sample, lift], axis=0)
        level_one = jax.nn.silu(stencil(framed(entry), w_enter, rows, cols) + bias_one).astype(jnp.bfloat16)
        level_two = jax.nn.silu(pooled(level_one, pool_fine) + bias_two).astype(jnp.bfloat16)
        level_three = jax.nn.silu(pooled(level_two, pool_mid) + bias_three).astype(jnp.bfloat16)
        return (level_one, level_two, level_three)
    deepest = lax.map(lambda pair: encode(pair)[2], (noisy, lifted))
    squeezed = jnp.einsum('ic,pchs->pihs', w_squeeze.astype(jnp.float32), deepest.astype(jnp.float32), precision=lax.Precision.HIGHEST).astype(jnp.bfloat16)
    planes = noisy.shape[0]
    beside_all = jnp.pad(squeezed, ((1, 1), (0, 0), (0, 0), (0, 0)))
    mixed = deepest.astype(jnp.float32)
    for tap in range(3):
        mixed = mixed + jnp.einsum('oi,pihs->pohs', w_across[tap].astype(jnp.float32), beside_all[tap:tap + planes].astype(jnp.float32), precision=lax.Precision.HIGHEST)
    mixed = mixed.astype(jnp.bfloat16)

    def decode(triple):
        sample, lift, middle = triple
        level_one, level_two, unused = encode((sample, lift))
        rows, cols = (sample.shape[1], sample.shape[2])
        coarse = jax.nn.silu(stencil(framed(middle), w_middle, rows // 4, cols // 4)).astype(jnp.bfloat16)
        joined_two = (raised(coarse, rise_mid) + level_two.astype(jnp.float32)).astype(jnp.bfloat16)
        decoded_two = jax.nn.silu(stencil(framed(joined_two), decode_mid, rows // 2, cols // 2)).astype(jnp.bfloat16)
        joined_one = (raised(decoded_two, rise_fine) + level_one.astype(jnp.float32)).astype(jnp.bfloat16)
        decoded_one = jax.nn.silu(stencil(framed(joined_one), decode_fine, rows, cols)).astype(jnp.bfloat16)
        return stencil(framed(decoded_one), w_leave, rows, cols).astype(jnp.bfloat16)
    noise_pred = lax.map(decode, (noisy, lifted, mixed))
    now = plan(timestep[0])
    prior = plan(timestep[0] - STRIDE)
    sample_f = noisy.astype(jnp.float32)
    guess = noise_pred.astype(jnp.float32)
    clean = (sample_f - jnp.sqrt(1.0 - now) * guess) / jnp.sqrt(now)
    next_sample = jnp.sqrt(prior) * clean + jnp.sqrt(1.0 - prior) * guess
    return (noise_pred, next_sample)
```

```python
import math

import jax
import jax.numpy as jnp
import numpy as np
from jax import lax
from jax.experimental import pallas as pl
from jax.experimental.pallas import tpu as pltpu
from jax.sharding import PartitionSpec as P

CF = 8
TSTEPS = 1000
STRIDE = 20
RIM = 9
EDGE = 2
BF = jnp.bfloat16
F32 = jnp.float32
AXES = ("plane", "span", "height")


def up(n, m):
    return -(-n // m) * m


def dot(a, b):
    return jnp.dot(a, b, preferred_element_type=F32)


def dot_nt(a, b):
    return lax.dot_general(a, b, (((1,), (1,)), ((), ())), preferred_element_type=F32)


def silu(x):
    half = 0.5 * x
    return half + half * jnp.tanh(half)


class Sizes:
    def __init__(self, rows, cols, planes, spans, heights, cond_rows, cond_cols):
        self.rows, self.cols = rows, cols
        self.planes, self.spans, self.heights = planes, spans, heights
        self.cond_rows, self.cond_cols = cond_rows, cond_cols
        self.devices = planes * spans * heights
        self.gi, self.gj = rows // 4 + 2 * EDGE, cols // 4 + 2 * EDGE
        self.step = up(self.gj, 16)
        self.cells = self.gi * self.step
        self.slots = min(planes, 3)
        self.strip = up(3 * RIM, 16)
        self.ext = 2 * self.strip + 3 * rows
        self.patch_rows, self.patch_cols = rows // CF + 4, cols // CF + 4
        self.patch = up(self.patch_rows, 16)
        self.piece = self.strip + self.patch * ((self.slots + 1) // 2)

    def planes_of(self, plane):
        if self.planes == 1:
            return [plane]
        if self.planes == 2:
            return [plane, 1 - plane]
        return [plane, plane - 1, plane + 1]


def pack_constants(z):
    bottom = np.zeros((z.strip, 3 * z.rows), np.float32)
    top = np.zeros((z.strip, 3 * z.rows), np.float32)
    for c in range(3):
        for r in range(RIM):
            bottom[c * RIM + r, c * z.rows + z.rows - RIM + r] = 1
            top[c * RIM + r, c * z.rows + r] = 1
    sides = np.zeros((2 * 16, z.cols), np.float32)
    for r in range(RIM):
        sides[r, z.cols - RIM + r] = 1
        sides[16 + r, r] = 1
    window = np.zeros((3, z.cond_cols, z.spans * 128), np.float32)
    for s in range(z.spans):
        for x in range(z.patch_cols):
            col = s * (z.cols // CF) + x - 2
            if 0 <= col < z.cond_cols:
                for c in range(3):
                    window[c, col, s * 128 + c * z.patch_cols + x] = 1
    return np.concatenate([bottom, top]).astype(BF), sides.astype(BF), window.astype(BF)


def unpack_constants(z):
    across = np.zeros((z.cols + 128, 6 * 64), np.float32)
    lift = np.zeros((2, 3, 128, 6 * 64), np.float32)
    for b in range(6):
        for j in range(z.gj):
            col = 4 * (j - EDGE) - 1 + b
            if col < 0:
                across[z.cols + 128 + col, b * 64 + j] = 1
            elif col < z.cols:
                across[col, b * 64 + j] = 1
            else:
                across[z.cols + col - z.cols, b * 64 + j] = 1
            for half in range(2):
                for c in range(3):
                    lift[half, c, half * 64 + c * z.patch_cols + col // CF + 2, b * 64 + j] = 1
    down = np.zeros((z.gi * 40, z.ext + 3 * z.patch), np.float32)
    for i in range(z.gi):
        for c in range(3):
            for a in range(6):
                row = 4 * (i - EDGE) - 1 + a
                if row < 0:
                    source = c * RIM + row + RIM
                elif row < z.rows:
                    source = z.strip + c * z.rows + row
                else:
                    source = z.strip + 3 * z.rows + c * RIM + row - z.rows
                down[i * 40 + c * 6 + a, source] = 1
                down[i * 40 + 18 + c * 6 + a, z.ext + c * z.patch + row // CF + 2] = 1
    sides = np.zeros((2 * 16, 128), np.float32)
    for r in range(RIM):
        sides[r, 128 - RIM + r] = 1
        sides[16 + r, r] = 1
    spread = np.zeros((2 * z.step, 2 * z.cols), np.float32)
    for pair in range(2):
        for j in range(z.cols // 4):
            for b in range(2):
                spread[pair * z.step + j + EDGE, b * z.cols + 4 * j + 2 * pair + b] = 1
    inner = z.rows // 4
    gather = np.zeros((2, 3 * z.rows, inner * 24), np.float32)
    for b in range(2):
        for i in range(inner):
            for a in range(4):
                for o in range(3):
                    gather[b, o * z.rows + 4 * i + a, i * 24 + a * 6 + b * 3 + o] = 1
    return tuple(
        m.astype(BF) for m in (across, lift.reshape(-1, 6 * 64), down, sides, spread, gather)
    )


def pack_kernel(z, noisy, slot, strips, sides, window, send, padded):
    plane, span, height = (lax.axis_index(a) for a in AXES)
    tile = noisy[0].reshape(3 * z.rows, z.cols)
    ends = dot(strips[...], tile).astype(BF)
    cols = dot_nt(sides[...], tile).astype(BF)
    wide = None
    for c in range(3):
        part = dot(slot[0, :, c].reshape(z.planes * z.cond_rows, z.cond_cols), window[c])
        wide = part if wide is None else wide + part
    padded[...] = jnp.zeros_like(padded)
    for p in range(z.planes):
        padded[p, 2 : 2 + z.cond_rows, :] = wide[p * z.cond_rows : (p + 1) * z.cond_rows]
    send[:, 0 : z.strip, :] = jnp.zeros((z.devices, z.strip, 128), BF)
    tall = z.rows // CF
    for p in range(z.planes):
        for s in range(z.spans):
            for h in range(z.heights):
                target = (p * z.spans + s) * z.heights + h
                for k0 in range(0, z.slots, 2):
                    both = None
                    for k in range(k0, min(k0 + 2, z.slots)):
                        q = z.planes_of(p)[k]
                        if 0 <= q < z.planes:
                            part = padded[
                                q, tall * h : tall * h + z.patch, s * 128 : (s + 1) * 128
                            ]
                            part = part if k == k0 else pltpu.roll(part, 64, 1)
                            both = part if both is None else both + part
                    if both is None:
                        both = jnp.zeros((z.patch, 128), F32)
                    base = z.strip + k0 // 2 * z.patch
                    send[target, base : base + z.patch, :] = both.astype(BF)
    for k in range(z.slots):
        q = z.planes_of(plane)[k]
        for dh in (-1, 0, 1):
            for ds in (-1, 0, 1):
                if dh == 0 and ds == 0:
                    continue
                ok = (
                    (q >= 0) & (q < z.planes)
                    & (span + ds >= 0) & (span + ds < z.spans)
                    & (height + dh >= 0) & (height + dh < z.heights)
                )

                @pl.when(ok)
                def _(q=q, dh=dh, ds=ds):
                    target = (q * z.spans + span + ds) * z.heights + height + dh
                    if dh != 0:
                        half = 0 if dh > 0 else z.strip
                        send[target, 0 : z.strip, :] = ends[half : half + z.strip]
                    else:
                        half = 0 if ds > 0 else 16
                        send[target, 0:16, :] = cols[half : half + 16, 0:128]
                        send[target, 16:32, 0:64] = cols[half : half + 16, 128:192]


def net_kernel(
    z, owner, coefs, noisy, others, recv, bias,
    across, lift, down, sides, spread, gather,
    w_in, w_pf, w_pm, w_sq, w_ac, w_mid, w_rm, w_dm, w_rf, w_df, w_lv,
    pred, sample,
    ext, grid, entry, h1, d1, d2, sq, mx, v2, v1, e1, last, mask, half, halfp,
):
    plane, span, height = (lax.axis_index(a) for a in AXES)
    step, gi = z.step, z.gi
    n1, n2, n3 = w_in.shape[1] // 16, w_pf.shape[1], w_pm.shape[1]
    inner = z.rows // 4

    shape = (gi, step, 128)
    row = lax.broadcasted_iota(jnp.int32, shape, 0) + (height * inner - EDGE)
    col = lax.broadcasted_iota(jnp.int32, shape, 1) + (span * (z.cols // 4) - EDGE)
    lane = lax.broadcasted_iota(jnp.int32, shape, 2)
    row_in = (row >= 0) & (row < z.heights * inner)
    wide = z.spans * (z.cols // 4)
    here = row_in & (col >= 0) & (col < wide)
    colp = col + jnp.where(lane >= n1, 1, 0)
    herep = row_in & (colp >= 0) & (colp < wide)
    mask[...] = jnp.where(here, 1.0, 0.0).reshape(z.cells, 128)
    half[...] = jnp.where(here, 0.5, 0.0).reshape(z.cells, 128)
    halfp[...] = jnp.where(herep, 0.5, 0.0).reshape(z.cells, 128)

    def masked(x, rows, ref=mask):
        m = ref[rows, :]
        return x * jnp.concatenate([m] * (x.shape[1] // 128), axis=1)

    lanes = lax.broadcasted_iota(jnp.int32, (z.strip, 128), 1)
    b1 = bias[:, 0:n1]
    b1 = jnp.concatenate([b1] * 4, axis=1)
    b2 = bias[:, n1 : n1 + n2]
    b3 = bias[:, n1 + n2 : n1 + n2 + n3]

    for k in range(z.slots):
        q = z.planes_of(plane)[k]

        def piece(dh, ds, q=q):
            ok = (
                (q >= 0) & (q < z.planes)
                & (span + ds >= 0) & (span + ds < z.spans)
                & (height + dh >= 0) & (height + dh < z.heights)
            )
            source = (q * z.spans + span + ds) * z.heights + height + dh
            source = jnp.clip(source, 0, z.devices - 1)
            value = recv[source, 0 : z.strip, :].astype(F32)
            return jnp.where(ok, value, 0.0)

        tile = (noisy[0] if k == 0 else others[k - 1]).reshape(3 * z.rows, z.cols)
        ext[z.strip : z.strip + 3 * z.rows, 0 : z.cols] = tile
        for dh, base in ((-1, 0), (1, z.strip + 3 * z.rows)):
            ext[base : base + z.strip, 0 : z.cols] = piece(dh, 0).astype(BF)
            left, right = piece(dh, -1), piece(dh, 1)
            rim = jnp.where(lanes >= 128 - RIM, left, jnp.where(lanes < RIM, right, 0.0))
            ext[base : base + z.strip, z.cols : z.cols + 128] = rim.astype(BF)
        left, right = piece(0, -1), piece(0, 1)
        halves = [
            jnp.concatenate([v[0:16], v[16:32]], axis=1) for v in (left, right)
        ]
        rims = jnp.concatenate(halves, axis=0)
        rims = jnp.transpose(rims)[0 : 3 * z.rows].astype(BF)
        ext[z.strip : z.strip + 3 * z.rows, z.cols : z.cols + 128] = dot(
            rims, sides[...]
        ).astype(BF)
        base = z.strip + k // 2 * z.patch
        patch = recv[owner[0], base : base + z.patch, :]
        wide_rows = [dot(ext[...], across[...]).astype(BF)]
        for c in range(3):
            at = (k % 2 * 3 + c) * 128
            wide_rows.append(dot(patch, lift[at : at + 128, :]).astype(BF))
        grid[...] = dot(down[...], jnp.concatenate(wide_rows, axis=0))
        for i in range(gi):
            block = grid[i * 40 : (i + 1) * 40, :]
            stack = jnp.concatenate(
                [block[:, 0:128], block[:, 128:256], block[:, 256:384], jnp.zeros((8, 128), F32)],
                axis=0,
            )
            turned = jnp.transpose(stack)
            at = i * step
            entry[at : at + step, 0:128] = turned[0:step].astype(BF)
            entry[at : at + step, 128:256] = turned[64 : 64 + step].astype(BF)
        per = 5 if gi % 5 == 0 else 1
        for i in range(0, gi, per):
            rows = slice(i * step, (i + per) * step)
            x = entry[rows, :]
            mids = []
            for g in range(4):
                h = dot(x, w_in[:, g * 4 * n1 : (g + 1) * 4 * n1]) + b1
                h = silu(h).astype(BF)
                if k == 0:
                    h1[g, rows, :] = h
                m = silu(dot(h, w_pf[...]) + b2).astype(BF)
                if k == 0:
                    d1[rows, g * n2 : (g + 1) * n2] = m
                mids.append(m)
            low = silu(dot(jnp.concatenate(mids, axis=1), w_pm[...]) + b3).astype(BF)
            if k == 0:
                d2[rows, :] = low
            width = w_sq.shape[1]
            sq[rows, k * width : (k + 1) * width] = dot(low, w_sq[...]).astype(BF)

    def chunks(first, last_, per):
        out = []
        while first < last_:
            out.append((first, min(per, last_ - first)))
            first += per
        return out

    def span_of(i, n, shift=0):
        return slice((i + shift) * step, (i + shift + n) * step)

    for i, n in chunks(0, gi, 5):
        rows = span_of(i, n)
        m = d2[rows, :].astype(F32) + dot(sq[rows, :], w_ac[...])
        m = masked(m, rows)
        mx[rows, n3 : 2 * n3] = m.astype(BF)
        mx[rows, 0:n3] = pltpu.roll(m, 1, 0).astype(BF)
        mx[rows, 2 * n3 : 3 * n3] = pltpu.roll(m, n * step - 1, 0).astype(BF)

    for i, n in chunks(1, gi - 1, 6):
        rows = span_of(i, n)
        c = None
        for a in range(3):
            part = dot(mx[span_of(i, n, a - 1), :], w_mid[a])
            c = part if c is None else c + part
        c = silu(c).astype(BF)
        v = dot(c, w_rm[...]) + d1[rows, :].astype(F32)
        v = masked(v, rows)
        for p in range(2):
            vp = v[:, 2 * p * n2 : 2 * (p + 1) * n2]
            v2[p, rows, n2 : 3 * n2] = vp.astype(BF)
            v2[p, rows, 0:n2] = pltpu.roll(vp[:, n2:], 1, 0).astype(BF)
            v2[p, rows, 3 * n2 : 4 * n2] = pltpu.roll(vp[:, :n2], n * step - 1, 0).astype(BF)

    for p in range(2):
        for i, n in chunks(2 - p, gi - 1 - p, 6):
            rows = span_of(i, n)
            e = None
            for a in range(3):
                at = p + a - 1
                part = dot(v2[at % 2, span_of(i, n, at // 2), :], w_dm[a])
                e = part if e is None else e + part
            e = silu(e).astype(BF)
            for q in range(2):
                v = dot(e[:, q * n2 : (q + 1) * n2], w_rf[...])
                v = masked(v + h1[2 * p + q, rows, :].astype(F32), rows)
                for a in range(2):
                    va = v[:, 2 * a * n1 : 2 * (a + 1) * n1]
                    v1[2 * p + a, rows, 2 * q * n1 : 2 * (q + 1) * n1] = va.astype(BF)
                    if q == 0:
                        v1[2 * p + a, rows, 4 * n1 : 6 * n1] = pltpu.roll(
                            va, n * step - 1, 0
                        ).astype(BF)

    for turn in range(2):
        for i, n in chunks(2 - turn, gi - 2, 6):
            rows = span_of(i, n)
            for pair in range(2):
                x = None
                for a in range(4):
                    at = 2 * turn + a
                    part = dot(
                        v1[at % 4, span_of(i, n, at // 4), 2 * pair * n1 : (2 * pair + 4) * n1],
                        w_df[a],
                    )
                    x = part if x is None else x + part
                for a in range(2):
                    at = 2 * turn + 1 + a
                    there = span_of(i, n, at // 4)
                    t = masked(
                        x[:, 2 * a * n1 : 2 * (a + 1) * n1], there, halfp if pair else half
                    )
                    t = t + t * jnp.tanh(t)
                    if pair == 0:
                        e1[at % 4, there, 2 * n1 : 4 * n1] = t.astype(BF)
                    else:
                        e1[at % 4, there, 4 * n1 : 6 * n1] = t.astype(BF)
                        e1[at % 4, there, 0 : 2 * n1] = pltpu.roll(t, 1, 0).astype(BF)

    for i, n in chunks(2, gi - 2, 8):
        outs = []
        for pair in range(2):
            x = None
            for a in range(6):
                at = a - 1
                part = dot(
                    e1[at % 4, span_of(i, n, at // 4), 2 * pair * n1 : (2 * pair + 4) * n1],
                    w_lv[a],
                )
                x = part if x is None else x + part
            outs.append(x)
        for r in range(n):
            block = jnp.concatenate([o[r * step : (r + 1) * step] for o in outs], axis=0)
            turned = jnp.transpose(block)[0:24]
            at = (i - 2 + r) * 24
            last[at : at + 24, :] = turned
    spread_out = dot(last[...].astype(BF), spread[...]).astype(BF)
    guess = dot(gather[0], spread_out[:, 0 : z.cols])
    guess = guess + dot(gather[1], spread_out[:, z.cols :])
    pred[0] = guess.astype(BF).reshape(3, z.rows, z.cols)
    given = noisy[0].reshape(3 * z.rows, z.cols).astype(F32)
    clean = (given - coefs[0] * guess) * coefs[1]
    result = coefs[2] * clean + coefs[3] * guess
    sample[0] = result.reshape(3, z.rows, z.cols)


def plan(stepnum):
    phase = (stepnum.astype(F32) / TSTEPS + 0.008) / 1.008 * (math.pi / 2.0)
    return jnp.cos(phase) ** 2


def time_bias(timestep, w_embed, w_biases):
    half = w_embed.shape[0] // 2
    freqs = jnp.exp(-math.log(10000.0) * jnp.arange(half, dtype=F32) / half)
    angles = timestep[0].astype(F32) * freqs
    waves = jnp.concatenate([jnp.sin(angles), jnp.cos(angles)])
    hidden = jax.nn.silu(jnp.dot(waves, w_embed, precision=lax.Precision.HIGHEST))
    return jnp.dot(hidden, w_biases, precision=lax.Precision.HIGHEST)


def lay_weights(
    z, plane, w_enter, pool_fine, pool_mid, w_squeeze, w_across, w_middle,
    rise_mid, decode_mid, rise_fine, decode_fine, w_leave,
):
    n1, n2, n3 = w_enter.shape[1], pool_fine.shape[1], pool_mid.shape[1]
    w = w_enter.reshape(3, n1, 3, 6).transpose(0, 2, 3, 1)
    parts = []
    for p in range(2):
        for q in range(2):
            for a in range(2):
                for b in range(2):
                    y, x = 2 * p + a, 2 * q + b
                    parts.append(jnp.pad(w, ((y, 3 - y), (x, 3 - x), (0, 0), (0, 0))))
    w = jnp.stack(parts, axis=3)
    w = w.reshape(6, 3, 2, 6, 16 * n1).transpose(2, 1, 3, 0, 4).reshape(2, 3, 36, 16 * n1)
    w = jnp.pad(w, ((0, 0), (0, 0), (0, 4), (0, 0))).reshape(2, 120, 16 * n1)
    w_in = jnp.pad(w, ((0, 0), (0, 8), (0, 0))).reshape(256, 16 * n1)
    w_pf = pool_fine.transpose(0, 2, 1).reshape(4 * n1, n2)
    w_pm = pool_mid.transpose(0, 2, 1).reshape(4 * n2, n3)
    taps = [w_across[1]]
    if z.planes == 2:
        taps.append(jnp.where(plane == 0, w_across[2], w_across[0]))
    elif z.planes > 2:
        taps.append(jnp.where(plane > 0, w_across[0], jnp.zeros_like(w_across[0])))
        taps.append(jnp.where(plane < z.planes - 1, w_across[2], jnp.zeros_like(w_across[2])))
    w_ac = jnp.concatenate([t.T for t in taps], axis=0)
    w_mid = w_middle.transpose(0, 2, 1)
    w_rm = rise_mid.transpose(2, 0, 1).reshape(n3, 4 * n2)
    w = decode_mid.transpose(0, 2, 1)
    w_dm = jnp.concatenate(
        [jnp.pad(w, ((0, 0), (q * n2, (1 - q) * n2), (0, 0))) for q in range(2)], axis=2
    )
    w_rf = rise_fine.transpose(2, 0, 1).reshape(n2, 4 * n1)
    w = decode_fine.transpose(0, 2, 1)
    w_df = jnp.concatenate(
        [
            jnp.pad(w, ((a, 1 - a), (b * n1, (1 - b) * n1), (0, 0)))
            for a in range(2)
            for b in range(2)
        ],
        axis=2,
    )
    w = w_leave.transpose(0, 2, 1)
    w_lv = jnp.concatenate(
        [
            jnp.pad(w, ((a, 3 - a), (b * n1, (1 - b) * n1), (0, 0)))
            for a in range(4)
            for b in range(2)
        ],
        axis=2,
    )
    w_lv = jnp.pad(w_lv, ((0, 0), (0, 0), (0, 128 - w_lv.shape[2])))
    return w_in, w_pf, w_pm, w_sq_t(w_squeeze), w_ac, w_mid, w_rm, w_dm, w_rf, w_df, w_lv


def w_sq_t(w_squeeze):
    return w_squeeze.T


def solution(mesh):
    planes, spans, heights = (mesh.shape[a] for a in AXES)

    def shards(
        noisy, coarse_cond, timestep, owner, w_embed, w_biases, w_enter, pool_fine, pool_mid,
        w_squeeze, w_across, w_middle, rise_mid, decode_mid, rise_fine, decode_fine, w_leave,
    ):
        rows, cols = noisy.shape[2:]
        z = Sizes(rows, cols, planes, spans, heights, *coarse_cond.shape[3:])
        n1, n2, n3 = w_enter.shape[1], pool_fine.shape[1], pool_mid.shape[1]
        vmem = pl.BlockSpec(memory_space=pltpu.VMEM)
        smem = pl.BlockSpec(memory_space=pltpu.SMEM)
        strips, sides, window = (jnp.asarray(m) for m in pack_constants(z))
        send = pl.pallas_call(
            lambda *refs: pack_kernel(z, *refs),
            out_shape=jax.ShapeDtypeStruct((z.devices, z.piece, 128), BF),
            in_specs=[vmem] * 5,
            out_specs=vmem,
            scratch_shapes=[
                pltpu.VMEM((planes, up(z.cond_rows + 4 + 8, 8), spans * 128), F32)
            ],
            compiler_params=pltpu.CompilerParams(vmem_limit_bytes=32 * 2**20),
            name="pack",
        )(noisy, coarse_cond, strips, sides, window)
        recv = lax.all_to_all(send, AXES, 0, 0, tiled=True)
        tile = noisy[0]
        if planes == 1:
            others = tile[None]
        elif planes == 2:
            others = lax.ppermute(tile, "plane", [(0, 1), (1, 0)])[None]
        else:
            ahead = [(i, i + 1) for i in range(planes - 1)]
            behind = [(i + 1, i) for i in range(planes - 1)]
            others = jnp.stack(
                [lax.ppermute(tile, "plane", ahead), lax.ppermute(tile, "plane", behind)]
            )
        plane = lax.axis_index("plane")
        bias = time_bias(timestep, w_embed, w_biases)[None]
        now, prior = plan(timestep[0]), plan(timestep[0] - STRIDE)
        coefs = jnp.stack(
            [jnp.sqrt(1.0 - now), 1.0 / jnp.sqrt(now), jnp.sqrt(prior), jnp.sqrt(1.0 - prior)]
        )
        weights = lay_weights(
            z, plane, w_enter, pool_fine, pool_mid, w_squeeze, w_across, w_middle,
            rise_mid, decode_mid, rise_fine, decode_fine, w_leave,
        )
        constants = [jnp.asarray(m) for m in unpack_constants(z)]
        operands = [owner, coefs, noisy, others, recv, bias, *constants, *weights]
        cells = z.cells
        return pl.pallas_call(
            lambda *refs: net_kernel(z, *refs),
            out_shape=(
                jax.ShapeDtypeStruct(noisy.shape, BF),
                jax.ShapeDtypeStruct(noisy.shape, F32),
            ),
            in_specs=[smem, smem] + [vmem] * (len(operands) - 2),
            out_specs=(vmem, vmem),
            scratch_shapes=[
                pltpu.VMEM((z.ext, cols + 128), BF),
                pltpu.VMEM((z.gi * 40, 384), F32),
                pltpu.VMEM((cells, 256), BF),
                pltpu.VMEM((4, cells, 4 * n1), BF),
                pltpu.VMEM((cells, 4 * n2), BF),
                pltpu.VMEM((cells, n3), BF),
                pltpu.VMEM((cells, z.slots * w_squeeze.shape[0]), BF),
                pltpu.VMEM((cells, 3 * n3), BF),
                pltpu.VMEM((2, cells, 4 * n2), BF),
                pltpu.VMEM((4, cells, 6 * n1), BF),
                pltpu.VMEM((4, cells, 6 * n1), BF),
                pltpu.VMEM((rows // 4 * 24, 2 * z.step), F32),
                pltpu.VMEM((cells, 128), F32),
                pltpu.VMEM((cells, 128), F32),
                pltpu.VMEM((cells, 128), F32),
            ],
            compiler_params=pltpu.CompilerParams(vmem_limit_bytes=48 * 2**20),
            name="net",
        )(*operands)

    copied = P()
    in_specs = (
        P("plane", None, "height", "span"),
        P(AXES, None, None, None, None),
    ) + (copied,) * 15
    out_specs = (P("plane", None, "height", "span"), P("plane", None, "height", "span"))
    return jax.shard_map(shards, mesh=mesh, in_specs=in_specs, out_specs=out_specs, check_vma=False)
```

```python
import math

import jax
import jax.numpy as jnp
import numpy as np
from jax import lax
from jax.experimental import pallas as pl
from jax.experimental.pallas import tpu as pltpu
from jax.sharding import PartitionSpec as P

CF = 8
TSTEPS = 1000
STRIDE = 20
RIM = 9
EDGE = 2
BF = jnp.bfloat16
F32 = jnp.float32
AXES = ("plane", "span", "height")


def up(n, m):
    return -(-n // m) * m


def dot(a, b):
    return jnp.dot(a, b, preferred_element_type=F32)


def dot_nt(a, b):
    return lax.dot_general(a, b, (((1,), (1,)), ((), ())), preferred_element_type=F32)


def silu(x):
    half = 0.5 * x
    return half + half * jnp.tanh(half)


class Sizes:
    def __init__(self, rows, cols, planes, spans, heights, cond_rows, cond_cols):
        self.rows, self.cols = rows, cols
        self.planes, self.spans, self.heights = planes, spans, heights
        self.cond_rows, self.cond_cols = cond_rows, cond_cols
        self.devices = planes * spans * heights
        self.gi, self.gj = rows // 4 + 2 * EDGE, cols // 4 + 2 * EDGE
        self.step = up(self.gj, 16)
        self.cells = self.gi * self.step
        self.slots = min(planes, 3)
        self.strip = up(3 * RIM, 16)
        self.ext = 2 * self.strip + 3 * rows
        self.patch_rows, self.patch_cols = rows // CF + 4, cols // CF + 4
        self.pairs = (self.slots + 1) // 2
        self.piece = up(3 * RIM + self.patch_rows * self.pairs, 8)
        self.pad = up(3 * RIM + self.patch_rows * self.pairs, 8)
        self.patch = up(self.piece, 16)

    def planes_of(self, plane):
        if self.planes == 1:
            return [plane]
        if self.planes == 2:
            return [plane, 1 - plane]
        return [plane, plane - 1, plane + 1]


def unpack_constants(z):
    across = np.zeros((z.cols + 128, 6 * 64), np.float32)
    lift = np.zeros((2, 3, 128, 6 * 64), np.float32)
    for b in range(6):
        for j in range(z.gj):
            col = 4 * (j - EDGE) - 1 + b
            if col < 0:
                across[z.cols + 128 + col, b * 64 + j] = 1
            elif col < z.cols:
                across[col, b * 64 + j] = 1
            else:
                across[z.cols + col - z.cols, b * 64 + j] = 1
            for half in range(2):
                for c in range(3):
                    lift[half, c, half * 64 + c * z.patch_cols + col // CF + 2, b * 64 + j] = 1
    down = np.zeros((z.pairs, z.gi * 40, z.ext + 3 * z.patch), np.float32)
    for i in range(z.gi):
        for c in range(3):
            for a in range(6):
                row = 4 * (i - EDGE) - 1 + a
                if row < 0:
                    source = c * RIM + row + RIM
                elif row < z.rows:
                    source = z.strip + c * z.rows + row
                else:
                    source = z.strip + 3 * z.rows + c * RIM + row - z.rows
                down[:, i * 40 + c * 6 + a, source] = 1
                for pair in range(z.pairs):
                    at = z.ext + c * z.patch + 3 * RIM + pair * z.patch_rows + row // CF + 2
                    down[pair, i * 40 + 18 + c * 6 + a, at] = 1
    sides = np.zeros((2 * 16, 128), np.float32)
    for r in range(RIM):
        sides[r, 128 - RIM + r] = 1
        sides[16 + r, r] = 1
    spread = np.zeros((2 * z.step, 2 * z.cols), np.float32)
    for pair in range(2):
        for j in range(z.cols // 4):
            for b in range(2):
                spread[pair * z.step + j + EDGE, b * z.cols + 4 * j + 2 * pair + b] = 1
    inner = z.rows // 4
    gather = np.zeros((2, 3 * z.rows, inner * 24), np.float32)
    for b in range(2):
        for i in range(inner):
            for a in range(4):
                for o in range(3):
                    gather[b, o * z.rows + 4 * i + a, i * 24 + a * 6 + b * 3 + o] = 1
    return tuple(
        m.astype(BF) for m in (across, lift.reshape(-1, 6 * 64), down, sides, spread, gather)
    )


def fetch(pairs, sems):
    copies = [
        pltpu.make_async_copy(source, target, sems.at[n])
        for n, (source, target) in enumerate(pairs)
    ]
    for copy in copies:
        copy.start()
    return copies


def pack_kernel(z, noisy_hbm, slot_hbm, send, noisy, slot, padded, sems):
    tile_copy, slot_copy = fetch(((noisy_hbm, noisy), (slot_hbm, slot)), sems)
    plane, span, height = (lax.axis_index(a) for a in AXES)
    tall, across = z.rows // CF, z.cols // CF

    shape = (z.cond_cols, z.spans * 128)
    col = lax.broadcasted_iota(jnp.int32, shape, 0)
    lane = lax.broadcasted_iota(jnp.int32, shape, 1)
    windows = []
    for c in range(3):
        x = (lane & 127) - c * z.patch_cols
        hit = (x >= 0) & (x < z.patch_cols) & (col == (lane >> 7) * across + x - 2)
        windows.append(jnp.where(hit, 1.0, 0.0).astype(BF))
    shape = (2 * z.strip, 3 * z.rows)
    row = lax.broadcasted_iota(jnp.int32, shape, 0)
    lane = lax.broadcasted_iota(jnp.int32, shape, 1)
    strips = jnp.zeros(shape, F32)
    for half, first in ((0, z.rows - RIM), (z.strip, 0)):
        for c in range(3):
            r = row - half - c * RIM
            hit = (r >= 0) & (r < RIM) & (lane == c * z.rows + first + r)
            strips = jnp.where(hit, 1.0, strips)
    strips = strips.astype(BF)
    shape = (32, z.cols)
    row = lax.broadcasted_iota(jnp.int32, shape, 0)
    lane = lax.broadcasted_iota(jnp.int32, shape, 1)
    hit = (row < RIM) & (lane == z.cols - RIM + row)
    hit = hit | ((row >= 16) & (row < 16 + RIM) & (lane == row - 16))
    sides = jnp.where(hit, 1.0, 0.0).astype(BF)

    base = 3 * RIM
    padded[...] = jnp.zeros_like(padded)
    slot_copy.wait()
    wide = None
    for c in range(3):
        part = dot(slot[0, :, c].reshape(z.planes * z.cond_rows, z.cond_cols), windows[c])
        wide = part if wide is None else wide + part
    for p in range(z.planes):
        at = z.pad + 2
        padded[p, at : at + z.cond_rows, :] = wide[p * z.cond_rows : (p + 1) * z.cond_rows]
    tile_copy.wait()
    tile = noisy[0].reshape(3 * z.rows, z.cols)
    ends = dot(strips, tile)
    cols = dot_nt(sides, tile)

    rows = lax.broadcasted_iota(jnp.int32, (z.piece, 128), 0)
    for p in range(z.planes):
        for s in range(z.spans):
            for h in range(z.heights):
                target = (p * z.spans + s) * z.heights + h
                total = jnp.zeros((z.piece, 128), F32)
                for k0 in range(0, z.slots, 2):
                    first = base + k0 // 2 * z.patch_rows
                    mine = (rows >= first) & (rows < first + z.patch_rows)
                    both = None
                    for k in range(k0, min(k0 + 2, z.slots)):
                        q = z.planes_of(p)[k]
                        if 0 <= q < z.planes:
                            at = z.pad + tall * h - first
                            part = padded[q, at : at + z.piece, s * 128 : (s + 1) * 128]
                            part = part if k == k0 else pltpu.roll(part, 64, 1)
                            both = part if both is None else both + part
                    if both is not None:
                        total = jnp.where(mine, both, total)
                send[target] = total.astype(BF)
    rest = jnp.zeros((z.piece - z.strip, 128), F32)
    blank = jnp.zeros((16, 128 - (3 * z.rows) % 128), F32)
    side = []
    for half in (0, 16):
        part = jnp.concatenate([cols[half : half + 16], blank], axis=1)
        side.append(
            jnp.concatenate([part[:, 0:128], part[:, 128:256], rest], axis=0)
        )
    ends = [
        jnp.concatenate([ends[half : half + z.strip], rest], axis=0) for half in (0, z.strip)
    ]
    for k in range(z.slots):
        q = z.planes_of(plane)[k]
        for dh in (-1, 0, 1):
            for ds in (-1, 0, 1):
                if dh == 0 and ds == 0:
                    continue
                ok = (
                    (q >= 0) & (q < z.planes)
                    & (span + ds >= 0) & (span + ds < z.spans)
                    & (height + dh >= 0) & (height + dh < z.heights)
                )

                @pl.when(ok)
                def _(q=q, dh=dh, ds=ds):
                    target = (q * z.spans + span + ds) * z.heights + height + dh
                    if dh != 0:
                        strip = ends[0 if dh > 0 else 1]
                    else:
                        strip = side[0 if ds > 0 else 1]
                    send[target] = (send[target].astype(F32) + strip).astype(BF)


def net_kernel(
    z, count, owner, noisy, others, recv, bias, *refs
):
    far, refs = refs[:count], refs[count:]
    pred, sample, refs = refs[0], refs[1], refs[2:]
    near, refs = refs[:count], refs[count:]
    ext, grid, entry, h1, d1, d2, sq, mx, v2, v1, e1, last, mask, half, halfp, sems = refs
    copies = fetch(tuple(zip(far, near)), sems)
    across, lift, down, sides, spread, gather = near[:6]
    w_in, w_pf, w_pm, w_sq, w_ac, w_mid, w_rm, w_dm, w_rf, w_df, w_lv = near[6:]
    plane, span, height = (lax.axis_index(a) for a in AXES)
    step, gi = z.step, z.gi
    n1, n2, n3 = w_in.shape[1] // 16, w_pf.shape[1], w_pm.shape[1]
    inner = z.rows // 4

    shape = (gi, step, 128)
    row = lax.broadcasted_iota(jnp.int32, shape, 0) + (height * inner - EDGE)
    col = lax.broadcasted_iota(jnp.int32, shape, 1) + (span * (z.cols // 4) - EDGE)
    lane = lax.broadcasted_iota(jnp.int32, shape, 2)
    row_in = (row >= 0) & (row < z.heights * inner)
    wide = z.spans * (z.cols // 4)
    here = row_in & (col >= 0) & (col < wide)
    colp = col + jnp.where(lane >= n1, 1, 0)
    herep = row_in & (colp >= 0) & (colp < wide)
    mask[...] = jnp.where(here, 1.0, 0.0).reshape(z.cells, 128)
    half[...] = jnp.where(here, 0.5, 0.0).reshape(z.cells, 128)
    halfp[...] = jnp.where(herep, 0.5, 0.0).reshape(z.cells, 128)

    def masked(x, rows, ref=mask):
        m = ref[rows, :]
        return x * jnp.concatenate([m] * (x.shape[1] // 128), axis=1)

    lanes = lax.broadcasted_iota(jnp.int32, (z.strip, 128), 1)
    b1 = bias[:, 0:n1]
    b1 = jnp.concatenate([b1] * 4, axis=1)
    b2 = bias[:, n1 : n1 + n2]
    b3 = bias[:, n1 + n2 : n1 + n2 + n3]

    for copy in copies[:4]:
        copy.wait()
    for k in range(z.slots):
        q = z.planes_of(plane)[k]

        def piece(dh, ds, q=q):
            ok = (
                (q >= 0) & (q < z.planes)
                & (span + ds >= 0) & (span + ds < z.spans)
                & (height + dh >= 0) & (height + dh < z.heights)
            )
            source = (q * z.spans + span + ds) * z.heights + height + dh
            source = jnp.clip(source, 0, z.devices - 1)
            value = recv[source].astype(F32)[0 : z.strip]
            return jnp.where(ok, value, 0.0)

        tile = (noisy[0] if k == 0 else others[k - 1]).reshape(3 * z.rows, z.cols)
        ext[z.strip : z.strip + 3 * z.rows, 0 : z.cols] = tile
        for dh, base in ((-1, 0), (1, z.strip + 3 * z.rows)):
            ext[base : base + z.strip, 0 : z.cols] = piece(dh, 0).astype(BF)
            left, right = piece(dh, -1), piece(dh, 1)
            rim = jnp.where(lanes >= 128 - RIM, left, jnp.where(lanes < RIM, right, 0.0))
            ext[base : base + z.strip, z.cols : z.cols + 128] = rim.astype(BF)
        left, right = piece(0, -1), piece(0, 1)
        halves = [
            jnp.concatenate([v[0:16], v[16:32]], axis=1) for v in (left, right)
        ]
        rims = jnp.concatenate(halves, axis=0)
        rims = jnp.transpose(rims)[0 : 3 * z.rows].astype(BF)
        ext[z.strip : z.strip + 3 * z.rows, z.cols : z.cols + 128] = dot(
            rims, sides[...]
        ).astype(BF)
        patch = recv[owner[0]].astype(F32)
        patch = jnp.concatenate([patch, jnp.zeros((z.patch - z.piece, 128), F32)], axis=0)
        patch = patch.astype(BF)
        wide_rows = [dot(ext[...], across[...]).astype(BF)]
        for c in range(3):
            at = (k % 2 * 3 + c) * 128
            wide_rows.append(dot(patch, lift[at : at + 128, :]).astype(BF))
        grid[...] = dot(down[k // 2], jnp.concatenate(wide_rows, axis=0))
        for i in range(gi):
            block = grid[i * 40 : (i + 1) * 40, :]
            stack = jnp.concatenate(
                [block[:, 0:128], block[:, 128:256], block[:, 256:384], jnp.zeros((8, 128), F32)],
                axis=0,
            )
            turned = jnp.transpose(stack)
            at = i * step
            entry[at : at + step, 0:128] = turned[0:step].astype(BF)
            entry[at : at + step, 128:256] = turned[64 : 64 + step].astype(BF)
        if k == 0:
            for copy in copies[6:10]:
                copy.wait()
        per = 5 if gi % 5 == 0 else 1
        for i in range(0, gi, per):
            rows = slice(i * step, (i + per) * step)
            x = entry[rows, :]
            mids = []
            for g in range(4):
                h = dot(x, w_in[:, g * 4 * n1 : (g + 1) * 4 * n1]) + b1
                h = silu(h).astype(BF)
                if k == 0:
                    h1[g, rows, :] = h
                m = silu(dot(h, w_pf[...]) + b2).astype(BF)
                if k == 0:
                    d1[rows, g * n2 : (g + 1) * n2] = m
                mids.append(m)
            low = silu(dot(jnp.concatenate(mids, axis=1), w_pm[...]) + b3).astype(BF)
            if k == 0:
                d2[rows, :] = low
            width = w_sq.shape[1]
            sq[rows, k * width : (k + 1) * width] = dot(low, w_sq[...]).astype(BF)

    def chunks(first, last_, per):
        out = []
        while first < last_:
            out.append((first, min(per, last_ - first)))
            first += per
        return out

    def span_of(i, n, shift=0):
        return slice((i + shift) * step, (i + shift + n) * step)

    for copy in copies[4:6] + copies[10:]:
        copy.wait()
    for i, n in chunks(0, gi, 5):
        rows = span_of(i, n)
        m = d2[rows, :].astype(F32) + dot(sq[rows, :], w_ac[...])
        m = masked(m, rows)
        mx[rows, n3 : 2 * n3] = m.astype(BF)
        mx[rows, 0:n3] = pltpu.roll(m, 1, 0).astype(BF)
        mx[rows, 2 * n3 : 3 * n3] = pltpu.roll(m, n * step - 1, 0).astype(BF)

    for i, n in chunks(1, gi - 1, 6):
        rows = span_of(i, n)
        c = None
        for a in range(3):
            part = dot(mx[span_of(i, n, a - 1), :], w_mid[a])
            c = part if c is None else c + part
        c = silu(c).astype(BF)
        v = dot(c, w_rm[...]) + d1[rows, :].astype(F32)
        v = masked(v, rows)
        for p in range(2):
            vp = v[:, 2 * p * n2 : 2 * (p + 1) * n2]
            v2[p, rows, n2 : 3 * n2] = vp.astype(BF)
            v2[p, rows, 0:n2] = pltpu.roll(vp[:, n2:], 1, 0).astype(BF)
            v2[p, rows, 3 * n2 : 4 * n2] = pltpu.roll(vp[:, :n2], n * step - 1, 0).astype(BF)

    for p in range(2):
        for i, n in chunks(2 - p, gi - 1 - p, 6):
            rows = span_of(i, n)
            e = None
            for a in range(3):
                at = p + a - 1
                part = dot(v2[at % 2, span_of(i, n, at // 2), :], w_dm[a])
                e = part if e is None else e + part
            e = silu(e).astype(BF)
            for q in range(2):
                v = dot(e[:, q * n2 : (q + 1) * n2], w_rf[...])
                v = masked(v + h1[2 * p + q, rows, :].astype(F32), rows)
                for a in range(2):
                    va = v[:, 2 * a * n1 : 2 * (a + 1) * n1]
                    v1[2 * p + a, rows, 2 * q * n1 : 2 * (q + 1) * n1] = va.astype(BF)
                    if q == 0:
                        v1[2 * p + a, rows, 4 * n1 : 6 * n1] = pltpu.roll(
                            va, n * step - 1, 0
                        ).astype(BF)

    for turn in range(2):
        for i, n in chunks(2 - turn, gi - 2, 6):
            rows = span_of(i, n)
            for pair in range(2):
                x = None
                for a in range(4):
                    at = 2 * turn + a
                    part = dot(
                        v1[at % 4, span_of(i, n, at // 4), 2 * pair * n1 : (2 * pair + 4) * n1],
                        w_df[a],
                    )
                    x = part if x is None else x + part
                for a in range(2):
                    at = 2 * turn + 1 + a
                    there = span_of(i, n, at // 4)
                    t = masked(
                        x[:, 2 * a * n1 : 2 * (a + 1) * n1], there, halfp if pair else half
                    )
                    t = t + t * jnp.tanh(t)
                    if pair == 0:
                        e1[at % 4, there, 2 * n1 : 4 * n1] = t.astype(BF)
                    else:
                        e1[at % 4, there, 4 * n1 : 6 * n1] = t.astype(BF)
                        e1[at % 4, there, 0 : 2 * n1] = pltpu.roll(t, 1, 0).astype(BF)

    for i, n in chunks(2, gi - 2, 8):
        outs = []
        for pair in range(2):
            x = None
            for a in range(6):
                at = a - 1
                part = dot(
                    e1[at % 4, span_of(i, n, at // 4), 2 * pair * n1 : (2 * pair + 4) * n1],
                    w_lv[a],
                )
                x = part if x is None else x + part
            outs.append(x)
        for r in range(n):
            block = jnp.concatenate([o[r * step : (r + 1) * step] for o in outs], axis=0)
            turned = jnp.transpose(block)[0:24]
            at = (i - 2 + r) * 24
            last[at : at + 24, :] = turned
    spread_out = dot(last[...].astype(BF), spread[...]).astype(BF)
    guess = dot(gather[0], spread_out[:, 0 : z.cols])
    guess = guess + dot(gather[1], spread_out[:, z.cols :])
    pred[0] = guess.astype(BF).reshape(3, z.rows, z.cols)
    given = noisy[0].reshape(3 * z.rows, z.cols).astype(F32)
    at = n1 + n2 + n3
    back, rise, keep, add = (bias[:, at + t : at + t + 1] for t in range(4))
    result = keep * ((given - back * guess) * rise) + add * guess
    sample[0] = result.reshape(3, z.rows, z.cols)


def plan(stepnum):
    phase = (stepnum.astype(F32) / TSTEPS + 0.008) / 1.008 * (math.pi / 2.0)
    return jnp.cos(phase) ** 2


def time_bias(timestep, w_embed, w_biases):
    half = w_embed.shape[0] // 2
    freqs = jnp.exp(-math.log(10000.0) * jnp.arange(half, dtype=F32) / half)
    angles = timestep[0].astype(F32) * freqs
    waves = jnp.concatenate([jnp.sin(angles), jnp.cos(angles)])
    hidden = jax.nn.silu(jnp.dot(waves, w_embed, precision=lax.Precision.HIGHEST))
    return jnp.dot(hidden, w_biases, precision=lax.Precision.HIGHEST)


def entry_constants():
    place = np.zeros((8, 256, 128), np.float32)
    for y in range(4):
        for pair in range(2):
            for h in range(2):
                for la in range(3):
                    for lb in range(3):
                        for cin in range(6):
                            a, b = y + la, 2 * pair + h + lb
                            row = b % 2 * 128 + b // 2 * 40 + cin * 6 + a
                            place[y * 2 + pair, row, h * 64 + la * 18 + lb * 6 + cin] = 1
    return place.astype(BF)


def lay_kernel(z, count, *refs):
    far, refs = refs[:count], refs[count:]
    tile, refs = refs[0], refs[1:]
    w_in, w_pm, w_sq, w_ac, w_mid, w_rm, w_dm, w_rf, w_df, w_lv = refs[:10]
    near, refs = refs[10 : 10 + count], refs[10 + count :]
    nat, tall, leave, enter, sems = refs
    copies = fetch(tuple(zip(far, near)), sems)
    (noisy, place, w_enter, w_leave, pool_mid, w_squeeze, w_across, w_middle,
     rise_mid, decode_mid, rise_fine, decode_fine) = near
    plane = lax.axis_index("plane")
    n1, n2, n3 = decode_fine.shape[1], decode_mid.shape[1], w_middle.shape[1]

    for copy in copies:
        copy.wait()
    tile[...] = noisy[0]
    tall[...] = jnp.zeros_like(tall)
    leave[...] = jnp.zeros_like(leave)
    enter[...] = jnp.zeros_like(enter)
    blank = jnp.zeros(w_enter.shape[1:], F32)
    for a in range(3):
        leave[3 * a : 3 * a + 3, 0 : 3 * n1] = w_leave[a].astype(F32)
        for h in range(2):
            taps = w_enter[a].astype(F32)
            taps = jnp.concatenate([blank, taps] if h else [taps, blank], axis=1)
            enter[h * n1 + a * 18 : h * n1 + a * 18 + 18, :] = taps
    turned = jnp.transpose(leave[...])[0 : 3 * n1].astype(BF)
    spots = enter[...].astype(BF)
    for b in range(2):
        tall[b, b * n1 : (b + 3) * n1, :] = turned
    line = lax.broadcasted_iota(jnp.int32, (128, 128), 0)
    lane = lax.broadcasted_iota(jnp.int32, (128, 128), 1)
    for y in range(6):
        total = None
        for b in range(2):
            pick = jnp.zeros((128, 128), F32)
            for a in range(4):
                if 0 <= y - a < 3:
                    o = lane - (6 * a + 3 * b)
                    hit = (o >= 0) & (o < 3) & (line == 3 * (y - a) + o)
                    pick = jnp.where(hit, 1.0, pick)
            part = dot(tall[b], pick.astype(BF))
            total = part if total is None else total + part
        w_lv[y] = total.astype(BF)

    for y in range(4):
        for pair in range(2):
            at = ((y // 2 * 2 + pair) * 2 + y % 2) * 2 * n1
            w_in[:, at : at + 2 * n1] = dot(place[y * 2 + pair], spots).astype(BF)
    for t in range(4):
        w_pm[t * n2 : (t + 1) * n2, :] = jnp.transpose(pool_mid[t])
        w_rm[:, t * n2 : (t + 1) * n2] = jnp.transpose(rise_mid[t])
    w_sq[...] = jnp.transpose(w_squeeze[...])
    width = w_across.shape[2]
    taps = [w_across[1]]
    zero = jnp.zeros_like(taps[0])
    if z.planes == 2:
        taps.append(jnp.where(plane == 0, w_across[2], w_across[0]))
    elif z.planes > 2:
        taps.append(jnp.where(plane > 0, w_across[0], zero))
        taps.append(jnp.where(plane < z.planes - 1, w_across[2], zero))
    for k, tap in enumerate(taps):
        w_ac[k * width : (k + 1) * width, :] = jnp.transpose(tap)
    for a in range(3):
        w_mid[a] = jnp.transpose(w_middle[a])
        turned = jnp.transpose(decode_mid[a])
        w_dm[a] = jnp.zeros((4 * n2, 2 * n2), BF)
        w_dm[a, 0 : 3 * n2, 0:n2] = turned
        w_dm[a, n2 : 4 * n2, n2 : 2 * n2] = turned
    w_rf[...] = jnp.transpose(rise_fine[...].reshape(4 * n1, n2))

    nat[...] = jnp.zeros_like(nat)
    for a in range(3):
        for b in range(2):
            wide = jnp.concatenate(
                [decode_fine[a].astype(F32), jnp.zeros((n1, n1), F32)], axis=1
            )
            wide = pltpu.roll(wide, b * n1, 1) if b else wide
            for r in range(2):
                nat[a + r, (2 * r + b) * n1 : (2 * r + b + 1) * n1, :] = wide.astype(BF)
    for a in range(4):
        w_df[a] = jnp.transpose(nat[a])


def solution(mesh):
    planes, spans, heights = (mesh.shape[a] for a in AXES)

    def shards(
        noisy, coarse_cond, timestep, owner, w_embed, w_biases, w_enter, pool_fine, pool_mid,
        w_squeeze, w_across, w_middle, rise_mid, decode_mid, rise_fine, decode_fine, w_leave,
    ):
        rows, cols = noisy.shape[2:]
        z = Sizes(rows, cols, planes, spans, heights, *coarse_cond.shape[3:])
        n1, n2, n3 = w_enter.shape[1], pool_fine.shape[1], pool_mid.shape[1]
        vmem = pl.BlockSpec(memory_space=pltpu.VMEM)
        smem = pl.BlockSpec(memory_space=pltpu.SMEM)
        far = pl.BlockSpec(memory_space=pltpu.HBM)
        send = pl.pallas_call(
            lambda *refs: pack_kernel(z, *refs),
            out_shape=jax.ShapeDtypeStruct((z.devices, z.piece, 128), BF),
            in_specs=[far] * 2,
            out_specs=vmem,
            scratch_shapes=[
                pltpu.VMEM(noisy.shape, BF),
                pltpu.VMEM(coarse_cond.shape, BF),
                pltpu.VMEM((planes, up(z.cond_rows, 8) + 2 * z.pad, spans * 128), F32),
                pltpu.SemaphoreType.DMA((2,)),
            ],
            compiler_params=pltpu.CompilerParams(vmem_limit_bytes=63 * 2**20),
            name="pack",
        )(noisy, coarse_cond)
        recv = lax.all_to_all(send, AXES, 0, 0, tiled=True)
        now, prior = plan(timestep[0]), plan(timestep[0] - STRIDE)
        coefs = jnp.stack(
            [jnp.sqrt(1.0 - now), 1.0 / jnp.sqrt(now), jnp.sqrt(prior), jnp.sqrt(1.0 - prior)]
        )
        bias = jnp.concatenate([time_bias(timestep, w_embed, w_biases), coefs])[None]
        raw = (
            noisy, jnp.asarray(entry_constants()), w_enter.transpose(0, 2, 1), w_leave, pool_mid,
            w_squeeze, w_across, w_middle, rise_mid, decode_mid, rise_fine, decode_fine,
        )
        inner = w_squeeze.shape[0]
        shapes = (
            noisy.shape[1:],
            (256, 16 * n1), (4 * n2, n3), (n3, inner), (z.slots * inner, n3),
            (3, 3 * n3, n3), (n3, 4 * n2), (3, 4 * n2, 2 * n2), (n2, 4 * n1),
            (4, 4 * n1, 4 * n1), (6, 4 * n1, 128),
        )
        tile, *weights = pl.pallas_call(
            lambda *refs: lay_kernel(z, len(raw), *refs),
            out_shape=tuple(jax.ShapeDtypeStruct(shape, BF) for shape in shapes),
            in_specs=[far] * len(raw),
            out_specs=(vmem,) * len(shapes),
            scratch_shapes=[pltpu.VMEM(w.shape, BF) for w in raw]
            + [
                pltpu.VMEM((4, 4 * n1, 4 * n1), BF),
                pltpu.VMEM((2, 4 * n1, 128), BF),
                pltpu.VMEM((128, 4 * n1), F32),
                pltpu.VMEM((2 * n1, 2 * n1), F32),
                pltpu.SemaphoreType.DMA((len(raw),)),
            ],
            compiler_params=pltpu.CompilerParams(vmem_limit_bytes=63 * 2**20),
            cost_estimate=pl.CostEstimate(
                flops=10**9, bytes_accessed=10**7, transcendentals=0
            ),
            name="lay",
        )(*raw)
        if planes == 1:
            others = tile[None]
        elif planes == 2:
            others = lax.ppermute(tile, "plane", [(0, 1), (1, 0)])[None]
        else:
            ahead = [(i, i + 1) for i in range(planes - 1)]
            behind = [(i + 1, i) for i in range(planes - 1)]
            others = jnp.stack(
                [lax.ppermute(tile, "plane", ahead), lax.ppermute(tile, "plane", behind)]
            )
        constants = [jnp.asarray(m) for m in unpack_constants(z)]
        w_pf = pool_fine.transpose(0, 2, 1).reshape(4 * n1, n2)
        operands = [*constants, weights[0], w_pf, *weights[1:]]
        cells = z.cells
        return pl.pallas_call(
            lambda *refs: net_kernel(z, len(operands), *refs),
            out_shape=(
                jax.ShapeDtypeStruct(noisy.shape, BF),
                jax.ShapeDtypeStruct(noisy.shape, F32),
            ),
            in_specs=[smem] + [vmem] * 4 + [far] * len(operands),
            out_specs=(vmem, vmem),
            scratch_shapes=[pltpu.VMEM(w.shape, BF) for w in operands]
            + [
                pltpu.VMEM((z.ext, cols + 128), BF),
                pltpu.VMEM((z.gi * 40, 384), F32),
                pltpu.VMEM((cells, 256), BF),
                pltpu.VMEM((4, cells, 4 * n1), BF),
                pltpu.VMEM((cells, 4 * n2), BF),
                pltpu.VMEM((cells, n3), BF),
                pltpu.VMEM((cells, z.slots * inner), BF),
                pltpu.VMEM((cells, 3 * n3), BF),
                pltpu.VMEM((2, cells, 4 * n2), BF),
                pltpu.VMEM((4, cells, 6 * n1), BF),
                pltpu.VMEM((4, cells, 6 * n1), BF),
                pltpu.VMEM((rows // 4 * 24, 2 * z.step), F32),
                pltpu.VMEM((cells, 128), F32),
                pltpu.VMEM((cells, 128), F32),
                pltpu.VMEM((cells, 128), F32),
                pltpu.SemaphoreType.DMA((len(operands),)),
            ],
            compiler_params=pltpu.CompilerParams(vmem_limit_bytes=63 * 2**20),
            name="net",
        )(owner, noisy, others, recv, bias, *operands)

    copied = P()
    in_specs = (
        P("plane", None, "height", "span"),
        P(AXES, None, None, None, None),
    ) + (copied,) * 15
    out_specs = (P("plane", None, "height", "span"), P("plane", None, "height", "span"))
    return jax.shard_map(shards, mesh=mesh, in_specs=in_specs, out_specs=out_specs, check_vma=False)
```

```python
import math

import jax
import jax.numpy as jnp
import numpy as np
from jax import lax
from jax.experimental import pallas as pl
from jax.experimental.pallas import tpu as pltpu
from jax.sharding import PartitionSpec as P

CF = 8
TSTEPS = 1000
STRIDE = 20
RIM = 9
EDGE = 2
BF = jnp.bfloat16
F32 = jnp.float32
AXES = ("plane", "span", "height")


def up(n, m):
    return -(-n // m) * m


def dot(a, b):
    return jnp.dot(a, b, preferred_element_type=F32)


def dot_nt(a, b):
    return lax.dot_general(a, b, (((1,), (1,)), ((), ())), preferred_element_type=F32)


def silu(x):
    half = 0.5 * x
    return half + half * jnp.tanh(half)


class Sizes:
    def __init__(self, rows, cols, planes, spans, heights, cond_rows, cond_cols):
        self.rows, self.cols = rows, cols
        self.planes, self.spans, self.heights = planes, spans, heights
        self.cond_rows, self.cond_cols = cond_rows, cond_cols
        self.devices = planes * spans * heights
        self.gi, self.gj = rows // 4 + 2 * EDGE, cols // 4 + 2 * EDGE
        self.step = up(self.gj, 16)
        self.cells = self.gi * self.step
        self.slots = min(planes, 3)
        self.strip = up(3 * RIM, 16)
        self.ext = 2 * self.strip + 3 * rows
        self.patch_rows, self.patch_cols = rows // CF + 4, cols // CF + 4
        self.pairs = (self.slots + 1) // 2
        self.piece = up(3 * RIM + self.patch_rows * self.pairs, 8)
        self.pad = up(3 * RIM + self.patch_rows * self.pairs, 8)
        self.patch = up(self.piece, 16)

    def planes_of(self, plane):
        if self.planes == 1:
            return [plane]
        if self.planes == 2:
            return [plane, 1 - plane]
        return [plane, plane - 1, plane + 1]


def unpack_constants(z):
    across = np.zeros((z.cols + 128, 6 * 64), np.float32)
    lift = np.zeros((2, 3, 128, 6 * 64), np.float32)
    for b in range(6):
        for j in range(z.gj):
            col = 4 * (j - EDGE) - 1 + b
            if col < 0:
                across[z.cols + 128 + col, b * 64 + j] = 1
            elif col < z.cols:
                across[col, b * 64 + j] = 1
            else:
                across[z.cols + col - z.cols, b * 64 + j] = 1
            for half in range(2):
                for c in range(3):
                    lift[half, c, half * 64 + c * z.patch_cols + col // CF + 2, b * 64 + j] = 1
    down = np.zeros((z.pairs, z.gi * 40, z.ext + 3 * z.patch), np.float32)
    for i in range(z.gi):
        for c in range(3):
            for a in range(6):
                row = 4 * (i - EDGE) - 1 + a
                if row < 0:
                    source = c * RIM + row + RIM
                elif row < z.rows:
                    source = z.strip + c * z.rows + row
                else:
                    source = z.strip + 3 * z.rows + c * RIM + row - z.rows
                down[:, i * 40 + c * 6 + a, source] = 1
                for pair in range(z.pairs):
                    at = z.ext + c * z.patch + 3 * RIM + pair * z.patch_rows + row // CF + 2
                    down[pair, i * 40 + 18 + c * 6 + a, at] = 1
    sides = np.zeros((2 * 16, 128), np.float32)
    for r in range(RIM):
        sides[r, 128 - RIM + r] = 1
        sides[16 + r, r] = 1
    spread = np.zeros((2 * z.step, 2 * z.cols), np.float32)
    for pair in range(2):
        for j in range(z.cols // 4):
            for b in range(2):
                spread[pair * z.step + j + EDGE, b * z.cols + 4 * j + 2 * pair + b] = 1
    inner = z.rows // 4
    gather = np.zeros((2, 3 * z.rows, inner * 24), np.float32)
    for b in range(2):
        for i in range(inner):
            for a in range(4):
                for o in range(3):
                    gather[b, o * z.rows + 4 * i + a, i * 24 + a * 6 + b * 3 + o] = 1
    return tuple(
        m.astype(BF) for m in (sides, across, lift.reshape(-1, 6 * 64), down, spread, gather)
    )


def fetch(pairs, sems):
    copies = [
        pltpu.make_async_copy(source, target, sems.at[n])
        for n, (source, target) in enumerate(pairs)
    ]
    for copy in copies:
        copy.start()
    return copies


def pack_kernel(z, noisy_hbm, slot_hbm, send, noisy, slot, padded, sems):
    tile_copy, slot_copy = fetch(((noisy_hbm, noisy), (slot_hbm, slot)), sems)
    plane, span, height = (lax.axis_index(a) for a in AXES)
    tall, across = z.rows // CF, z.cols // CF

    shape = (z.cond_cols, z.spans * 128)
    col = lax.broadcasted_iota(jnp.int32, shape, 0)
    lane = lax.broadcasted_iota(jnp.int32, shape, 1)
    windows = []
    for c in range(3):
        x = (lane & 127) - c * z.patch_cols
        hit = (x >= 0) & (x < z.patch_cols) & (col == (lane >> 7) * across + x - 2)
        windows.append(jnp.where(hit, 1.0, 0.0).astype(BF))
    shape = (2 * z.strip, 3 * z.rows)
    row = lax.broadcasted_iota(jnp.int32, shape, 0)
    lane = lax.broadcasted_iota(jnp.int32, shape, 1)
    strips = jnp.zeros(shape, F32)
    for half, first in ((0, z.rows - RIM), (z.strip, 0)):
        for c in range(3):
            r = row - half - c * RIM
            hit = (r >= 0) & (r < RIM) & (lane == c * z.rows + first + r)
            strips = jnp.where(hit, 1.0, strips)
    strips = strips.astype(BF)
    shape = (32, z.cols)
    row = lax.broadcasted_iota(jnp.int32, shape, 0)
    lane = lax.broadcasted_iota(jnp.int32, shape, 1)
    hit = (row < RIM) & (lane == z.cols - RIM + row)
    hit = hit | ((row >= 16) & (row < 16 + RIM) & (lane == row - 16))
    sides = jnp.where(hit, 1.0, 0.0).astype(BF)

    base = 3 * RIM
    padded[...] = jnp.zeros_like(padded)
    slot_copy.wait()
    wide = None
    for c in range(3):
        part = dot(slot[0, :, c].reshape(z.planes * z.cond_rows, z.cond_cols), windows[c])
        wide = part if wide is None else wide + part
    for p in range(z.planes):
        at = z.pad + 2
        padded[p, at : at + z.cond_rows, :] = wide[p * z.cond_rows : (p + 1) * z.cond_rows]
    tile_copy.wait()
    tile = noisy[0].reshape(3 * z.rows, z.cols)
    ends = dot(strips, tile)
    cols = dot_nt(sides, tile)

    rows = lax.broadcasted_iota(jnp.int32, (z.piece, 128), 0)
    for p in range(z.planes):
        for s in range(z.spans):
            for h in range(z.heights):
                target = (p * z.spans + s) * z.heights + h
                total = jnp.zeros((z.piece, 128), F32)
                for k0 in range(0, z.slots, 2):
                    first = base + k0 // 2 * z.patch_rows
                    mine = (rows >= first) & (rows < first + z.patch_rows)
                    both = None
                    for k in range(k0, min(k0 + 2, z.slots)):
                        q = z.planes_of(p)[k]
                        if 0 <= q < z.planes:
                            at = z.pad + tall * h - first
                            part = padded[q, at : at + z.piece, s * 128 : (s + 1) * 128]
                            part = part if k == k0 else pltpu.roll(part, 64, 1)
                            both = part if both is None else both + part
                    if both is not None:
                        total = jnp.where(mine, both, total)
                send[target] = total.astype(BF)
    rest = jnp.zeros((z.piece - z.strip, 128), F32)
    blank = jnp.zeros((16, 128 - (3 * z.rows) % 128), F32)
    side = []
    for half in (0, 16):
        part = jnp.concatenate([cols[half : half + 16], blank], axis=1)
        side.append(
            jnp.concatenate([part[:, 0:128], part[:, 128:256], rest], axis=0)
        )
    ends = [
        jnp.concatenate([ends[half : half + z.strip], rest], axis=0) for half in (0, z.strip)
    ]
    for k in range(z.slots):
        q = z.planes_of(plane)[k]
        for dh in (-1, 0, 1):
            for ds in (-1, 0, 1):
                if dh == 0 and ds == 0:
                    continue
                ok = (
                    (q >= 0) & (q < z.planes)
                    & (span + ds >= 0) & (span + ds < z.spans)
                    & (height + dh >= 0) & (height + dh < z.heights)
                )

                @pl.when(ok)
                def _(q=q, dh=dh, ds=ds):
                    target = (q * z.spans + span + ds) * z.heights + height + dh
                    if dh != 0:
                        strip = ends[0 if dh > 0 else 1]
                    else:
                        strip = side[0 if ds > 0 else 1]
                    send[target] = (send[target].astype(F32) + strip).astype(BF)


def net_kernel(
    z, count, owner, recv, others, *refs
):
    far, refs = refs[:count], refs[count:]
    pred_far, sample_far, refs = refs[0], refs[1], refs[2:]
    near, refs = refs[:count], refs[count:]
    (pred, sample, ext, grid, entry, h1, d1, d2, sq, mx, v2, v1, e1, last,
     mask, half, halfp, sems, out_sems) = refs
    copies = fetch(tuple(zip(far, near)), sems)
    noisy, sides, across, lift, down, bias = near[:6]
    w_in, w_pf, w_pm, w_sq, w_ac, w_mid, w_rm, w_dm, w_rf, w_df, w_lv, spread, gather = near[6:]
    plane, span, height = (lax.axis_index(a) for a in AXES)
    step, gi = z.step, z.gi
    n1, n2, n3 = w_in.shape[1] // 16, w_pf.shape[1], w_pm.shape[1]
    inner = z.rows // 4

    shape = (gi, step, 128)
    row = lax.broadcasted_iota(jnp.int32, shape, 0) + (height * inner - EDGE)
    col = lax.broadcasted_iota(jnp.int32, shape, 1) + (span * (z.cols // 4) - EDGE)
    lane = lax.broadcasted_iota(jnp.int32, shape, 2)
    row_in = (row >= 0) & (row < z.heights * inner)
    wide = z.spans * (z.cols // 4)
    here = row_in & (col >= 0) & (col < wide)
    colp = col + jnp.where(lane >= n1, 1, 0)
    herep = row_in & (colp >= 0) & (colp < wide)
    mask[...] = jnp.where(here, 1.0, 0.0).reshape(z.cells, 128)
    half[...] = jnp.where(here, 0.5, 0.0).reshape(z.cells, 128)
    halfp[...] = jnp.where(herep, 0.5, 0.0).reshape(z.cells, 128)

    def masked(x, rows, ref=mask):
        m = ref[rows, :]
        return x * jnp.concatenate([m] * (x.shape[1] // 128), axis=1)

    lanes = lax.broadcasted_iota(jnp.int32, (z.strip, 128), 1)
    for copy in copies[:5]:
        copy.wait()
    for k in range(z.slots):
        q = z.planes_of(plane)[k]

        def piece(dh, ds, q=q):
            ok = (
                (q >= 0) & (q < z.planes)
                & (span + ds >= 0) & (span + ds < z.spans)
                & (height + dh >= 0) & (height + dh < z.heights)
            )
            source = (q * z.spans + span + ds) * z.heights + height + dh
            source = jnp.clip(source, 0, z.devices - 1)
            value = recv[source].astype(F32)[0 : z.strip]
            return jnp.where(ok, value, 0.0)

        tile = (noisy[0] if k == 0 else others[k - 1]).reshape(3 * z.rows, z.cols)
        ext[z.strip : z.strip + 3 * z.rows, 0 : z.cols] = tile
        for dh, base in ((-1, 0), (1, z.strip + 3 * z.rows)):
            ext[base : base + z.strip, 0 : z.cols] = piece(dh, 0).astype(BF)
            left, right = piece(dh, -1), piece(dh, 1)
            rim = jnp.where(lanes >= 128 - RIM, left, jnp.where(lanes < RIM, right, 0.0))
            ext[base : base + z.strip, z.cols : z.cols + 128] = rim.astype(BF)
        left, right = piece(0, -1), piece(0, 1)
        halves = [
            jnp.concatenate([v[0:16], v[16:32]], axis=1) for v in (left, right)
        ]
        rims = jnp.concatenate(halves, axis=0)
        rims = jnp.transpose(rims)[0 : 3 * z.rows].astype(BF)
        ext[z.strip : z.strip + 3 * z.rows, z.cols : z.cols + 128] = dot(
            rims, sides[...]
        ).astype(BF)
        patch = recv[owner[0]].astype(F32)
        patch = jnp.concatenate([patch, jnp.zeros((z.patch - z.piece, 128), F32)], axis=0)
        patch = patch.astype(BF)
        wide_rows = [dot(ext[...], across[...]).astype(BF)]
        for c in range(3):
            at = (k % 2 * 3 + c) * 128
            wide_rows.append(dot(patch, lift[at : at + 128, :]).astype(BF))
        grid[...] = dot(down[k // 2], jnp.concatenate(wide_rows, axis=0))
        for i in range(gi):
            block = grid[i * 40 : (i + 1) * 40, :]
            stack = jnp.concatenate(
                [block[:, 0:128], block[:, 128:256], block[:, 256:384], jnp.zeros((8, 128), F32)],
                axis=0,
            )
            turned = jnp.transpose(stack)
            at = i * step
            entry[at : at + step, 0:128] = turned[0:step].astype(BF)
            entry[at : at + step, 128:256] = turned[64 : 64 + step].astype(BF)
        if k == 0:
            for copy in copies[5:10]:
                copy.wait()
            b1 = bias[:, 0:n1]
            b1 = jnp.concatenate([b1] * 4, axis=1)
            b2 = bias[:, n1 : n1 + n2]
            b3 = bias[:, n1 + n2 : n1 + n2 + n3]
        per = gi
        for i in range(0, gi, per):
            rows = slice(i * step, (i + per) * step)
            x = entry[rows, :]
            mids = []
            for g in range(4):
                h = dot(x, w_in[:, g * 4 * n1 : (g + 1) * 4 * n1]) + b1
                h = silu(h).astype(BF)
                if k == 0:
                    h1[g, rows, :] = h
                m = silu(dot(h, w_pf[...]) + b2).astype(BF)
                if k == 0:
                    d1[rows, g * n2 : (g + 1) * n2] = m
                mids.append(m)
            low = silu(dot(jnp.concatenate(mids, axis=1), w_pm[...]) + b3).astype(BF)
            if k == 0:
                d2[rows, :] = low
            width = w_sq.shape[1]
            sq[rows, k * width : (k + 1) * width] = dot(low, w_sq[...]).astype(BF)

    def chunks(first, last_, per):
        out = []
        while first < last_:
            out.append((first, min(per, last_ - first)))
            first += per
        return out

    def span_of(i, n, shift=0):
        return slice((i + shift) * step, (i + shift + n) * step)

    for copy in copies[10:]:
        copy.wait()
    for i, n in chunks(0, gi, 5):
        rows = span_of(i, n)
        m = d2[rows, :].astype(F32) + dot(sq[rows, :], w_ac[...])
        m = masked(m, rows)
        mx[rows, n3 : 2 * n3] = m.astype(BF)
        mx[rows, 0:n3] = pltpu.roll(m, 1, 0).astype(BF)
        mx[rows, 2 * n3 : 3 * n3] = pltpu.roll(m, n * step - 1, 0).astype(BF)

    for i, n in chunks(1, gi - 1, 18):
        rows = span_of(i, n)
        wide = [mx[span_of(i, n, a - 1), :] for a in range(3)]
        c = silu(dot(jnp.concatenate(wide, axis=1), w_mid[...])).astype(BF)
        v = dot(c, w_rm[...]) + d1[rows, :].astype(F32)
        v = masked(v, rows)
        for p in range(2):
            vp = v[:, 2 * p * n2 : 2 * (p + 1) * n2]
            v2[p, rows, n2 : 3 * n2] = vp.astype(BF)
            v2[p, rows, 0:n2] = pltpu.roll(vp[:, n2:], 1, 0).astype(BF)
            v2[p, rows, 3 * n2 : 4 * n2] = pltpu.roll(vp[:, :n2], n * step - 1, 0).astype(BF)

    for p in range(2):
        for i, n in chunks(2 - p, gi - 1 - p, 17):
            rows = span_of(i, n)
            wide = [
                v2[at % 2, span_of(i, n, at // 2), :] for at in range(p - 1, p + 2)
            ]
            e = silu(dot(jnp.concatenate(wide, axis=1), w_dm[...])).astype(BF)
            for q in range(2):
                v = dot(e[:, q * n2 : (q + 1) * n2], w_rf[...])
                v = masked(v + h1[2 * p + q, rows, :].astype(F32), rows)
                for a in range(2):
                    va = v[:, 2 * a * n1 : 2 * (a + 1) * n1]
                    v1[2 * p + a, rows, 2 * q * n1 : 2 * (q + 1) * n1] = va.astype(BF)
                    if q == 0:
                        v1[2 * p + a, rows, 4 * n1 : 6 * n1] = pltpu.roll(
                            va, n * step - 1, 0
                        ).astype(BF)

    for turn in range(2):
        for i, n in chunks(2 - turn, gi - 2, 6):
            rows = span_of(i, n)
            for pair in range(2):
                lanes_in = slice(2 * pair * n1, (2 * pair + 4) * n1)
                wide = [
                    v1[at % 4, span_of(i, n, at // 4), lanes_in]
                    for at in range(2 * turn, 2 * turn + 4)
                ]
                x = dot(jnp.concatenate(wide, axis=1), w_df[...])
                for a in range(2):
                    at = 2 * turn + 1 + a
                    there = span_of(i, n, at // 4)
                    t = masked(
                        x[:, 2 * a * n1 : 2 * (a + 1) * n1], there, halfp if pair else half
                    )
                    t = t + t * jnp.tanh(t)
                    if pair == 0:
                        e1[at % 4, there, 2 * n1 : 4 * n1] = t.astype(BF)
                    else:
                        e1[at % 4, there, 4 * n1 : 6 * n1] = t.astype(BF)
                        e1[at % 4, there, 0 : 2 * n1] = pltpu.roll(t, 1, 0).astype(BF)

    for i, n in chunks(2, gi - 2, 8):
        outs = []
        for pair in range(2):
            lanes_in = slice(2 * pair * n1, (2 * pair + 4) * n1)
            wide = [e1[at % 4, span_of(i, n, at // 4), lanes_in] for at in range(-1, 5)]
            outs.append(dot(jnp.concatenate(wide, axis=1), w_lv[...]))
        for r in range(n):
            block = jnp.concatenate([o[r * step : (r + 1) * step] for o in outs], axis=0)
            turned = jnp.transpose(block)[0:24]
            at = (i - 2 + r) * 24
            last[at : at + 24, :] = turned
    spread_out = dot(last[...].astype(BF), spread[...]).astype(BF)
    guess = dot(gather[0], spread_out[:, 0 : z.cols])
    guess = guess + dot(gather[1], spread_out[:, z.cols :])
    pred[0] = guess.astype(BF).reshape(3, z.rows, z.cols)
    pred_copy = pltpu.make_async_copy(pred, pred_far, out_sems.at[0])
    pred_copy.start()
    given = noisy[0].reshape(3 * z.rows, z.cols).astype(F32)
    at = n1 + n2 + n3
    back, rise, keep, add = (bias[:, at + t : at + t + 1] for t in range(4))
    result = keep * ((given - back * guess) * rise) + add * guess
    sample[0] = result.reshape(3, z.rows, z.cols)
    sample_copy = pltpu.make_async_copy(sample, sample_far, out_sems.at[1])
    sample_copy.start()
    pred_copy.wait()
    sample_copy.wait()


def plan(stepnum):
    phase = (stepnum.astype(F32) / TSTEPS + 0.008) / 1.008 * (math.pi / 2.0)
    return jnp.cos(phase) ** 2


def time_bias(timestep, w_embed, w_biases):
    half = w_embed.shape[0] // 2
    freqs = jnp.exp(-math.log(10000.0) * jnp.arange(half, dtype=F32) / half)
    angles = timestep[0].astype(F32) * freqs
    waves = jnp.concatenate([jnp.sin(angles), jnp.cos(angles)])
    hidden = jax.nn.silu(jnp.dot(waves, w_embed, precision=lax.Precision.HIGHEST))
    return jnp.dot(hidden, w_biases, precision=lax.Precision.HIGHEST)


def entry_constants():
    place = np.zeros((8, 256, 128), np.float32)
    for y in range(4):
        for pair in range(2):
            for h in range(2):
                for la in range(3):
                    for lb in range(3):
                        for cin in range(6):
                            a, b = y + la, 2 * pair + h + lb
                            row = b % 2 * 128 + b // 2 * 40 + cin * 6 + a
                            place[y * 2 + pair, row, h * 64 + la * 18 + lb * 6 + cin] = 1
    return place.astype(BF)


def lay_kernel(z, count, *refs):
    far, refs = refs[:count], refs[count:]
    tile, refs = refs[0], refs[1:]
    w_in, w_pm, w_sq, w_ac, w_mid, w_rm, w_dm, w_rf, w_df, w_lv = refs[:10]
    near, refs = refs[10 : 10 + count], refs[10 + count :]
    nat, tall, leave, enter, sems = refs
    copies = fetch(tuple(zip(far, near)), sems)
    (noisy, place, w_enter, w_leave, pool_mid, w_squeeze, w_across, w_middle,
     rise_mid, decode_mid, rise_fine, decode_fine) = near
    plane = lax.axis_index("plane")
    n1, n2, n3 = decode_fine.shape[1], decode_mid.shape[1], w_middle.shape[1]

    for copy in copies:
        copy.wait()
    tile[...] = noisy[0]
    tall[...] = jnp.zeros_like(tall)
    leave[...] = jnp.zeros_like(leave)
    enter[...] = jnp.zeros_like(enter)
    blank = jnp.zeros(w_enter.shape[1:], F32)
    for a in range(3):
        leave[3 * a : 3 * a + 3, 0 : 3 * n1] = w_leave[a].astype(F32)
        for h in range(2):
            taps = w_enter[a].astype(F32)
            taps = jnp.concatenate([blank, taps] if h else [taps, blank], axis=1)
            enter[h * n1 + a * 18 : h * n1 + a * 18 + 18, :] = taps
    turned = jnp.transpose(leave[...])[0 : 3 * n1].astype(BF)
    spots = enter[...].astype(BF)
    for b in range(2):
        tall[b, b * n1 : (b + 3) * n1, :] = turned
    line = lax.broadcasted_iota(jnp.int32, (128, 128), 0)
    lane = lax.broadcasted_iota(jnp.int32, (128, 128), 1)
    for y in range(6):
        total = None
        for b in range(2):
            pick = jnp.zeros((128, 128), F32)
            for a in range(4):
                if 0 <= y - a < 3:
                    o = lane - (6 * a + 3 * b)
                    hit = (o >= 0) & (o < 3) & (line == 3 * (y - a) + o)
                    pick = jnp.where(hit, 1.0, pick)
            part = dot(tall[b], pick.astype(BF))
            total = part if total is None else total + part
        w_lv[y * 4 * n1 : (y + 1) * 4 * n1, :] = total.astype(BF)

    for y in range(4):
        for pair in range(2):
            at = ((y // 2 * 2 + pair) * 2 + y % 2) * 2 * n1
            w_in[:, at : at + 2 * n1] = dot(place[y * 2 + pair], spots).astype(BF)
    for t in range(4):
        w_pm[t * n2 : (t + 1) * n2, :] = jnp.transpose(pool_mid[t])
        w_rm[:, t * n2 : (t + 1) * n2] = jnp.transpose(rise_mid[t])
    w_sq[...] = jnp.transpose(w_squeeze[...])
    width = w_across.shape[2]
    taps = [w_across[1]]
    zero = jnp.zeros_like(taps[0])
    if z.planes == 2:
        taps.append(jnp.where(plane == 0, w_across[2], w_across[0]))
    elif z.planes > 2:
        taps.append(jnp.where(plane > 0, w_across[0], zero))
        taps.append(jnp.where(plane < z.planes - 1, w_across[2], zero))
    for k, tap in enumerate(taps):
        w_ac[k * width : (k + 1) * width, :] = jnp.transpose(tap)
    for a in range(3):
        w_mid[a * 3 * n3 : (a + 1) * 3 * n3, :] = jnp.transpose(w_middle[a])
        turned = jnp.transpose(decode_mid[a])
        at = a * 4 * n2
        w_dm[at : at + 4 * n2, :] = jnp.zeros((4 * n2, 2 * n2), BF)
        w_dm[at : at + 3 * n2, 0:n2] = turned
        w_dm[at + n2 : at + 4 * n2, n2 : 2 * n2] = turned
    w_rf[...] = jnp.transpose(rise_fine[...].reshape(4 * n1, n2))

    nat[...] = jnp.zeros_like(nat)
    for a in range(3):
        for b in range(2):
            wide = jnp.concatenate(
                [decode_fine[a].astype(F32), jnp.zeros((n1, n1), F32)], axis=1
            )
            wide = pltpu.roll(wide, b * n1, 1) if b else wide
            for r in range(2):
                nat[a + r, (2 * r + b) * n1 : (2 * r + b + 1) * n1, :] = wide.astype(BF)
    for a in range(4):
        w_df[a * 4 * n1 : (a + 1) * 4 * n1, :] = jnp.transpose(nat[a])


def solution(mesh):
    planes, spans, heights = (mesh.shape[a] for a in AXES)

    def shards(
        noisy, coarse_cond, timestep, owner, w_embed, w_biases, w_enter, pool_fine, pool_mid,
        w_squeeze, w_across, w_middle, rise_mid, decode_mid, rise_fine, decode_fine, w_leave,
    ):
        rows, cols = noisy.shape[2:]
        z = Sizes(rows, cols, planes, spans, heights, *coarse_cond.shape[3:])
        n1, n2, n3 = w_enter.shape[1], pool_fine.shape[1], pool_mid.shape[1]
        vmem = pl.BlockSpec(memory_space=pltpu.VMEM)
        smem = pl.BlockSpec(memory_space=pltpu.SMEM)
        far = pl.BlockSpec(memory_space=pltpu.HBM)
        send = pl.pallas_call(
            lambda *refs: pack_kernel(z, *refs),
            out_shape=jax.ShapeDtypeStruct((z.devices, z.piece, 128), BF),
            in_specs=[far] * 2,
            out_specs=vmem,
            scratch_shapes=[
                pltpu.VMEM(noisy.shape, BF),
                pltpu.VMEM(coarse_cond.shape, BF),
                pltpu.VMEM((planes, up(z.cond_rows, 8) + 2 * z.pad, spans * 128), F32),
                pltpu.SemaphoreType.DMA((2,)),
            ],
            compiler_params=pltpu.CompilerParams(vmem_limit_bytes=63 * 2**20),
            name="pack",
        )(noisy, coarse_cond)
        recv = lax.all_to_all(send, AXES, 0, 0, tiled=True)
        now, prior = plan(timestep[0]), plan(timestep[0] - STRIDE)
        coefs = jnp.stack(
            [jnp.sqrt(1.0 - now), 1.0 / jnp.sqrt(now), jnp.sqrt(prior), jnp.sqrt(1.0 - prior)]
        )
        bias = jnp.concatenate([time_bias(timestep, w_embed, w_biases), coefs])[None]
        raw = (
            noisy, jnp.asarray(entry_constants()), w_enter.transpose(0, 2, 1), w_leave, pool_mid,
            w_squeeze, w_across, w_middle, rise_mid, decode_mid, rise_fine, decode_fine,
        )
        inner = w_squeeze.shape[0]
        shapes = (
            noisy.shape[1:],
            (256, 16 * n1), (4 * n2, n3), (n3, inner), (z.slots * inner, n3),
            (9 * n3, n3), (n3, 4 * n2), (12 * n2, 2 * n2), (n2, 4 * n1),
            (16 * n1, 4 * n1), (24 * n1, 128),
        )
        tile, *weights = pl.pallas_call(
            lambda *refs: lay_kernel(z, len(raw), *refs),
            out_shape=tuple(jax.ShapeDtypeStruct(shape, BF) for shape in shapes),
            in_specs=[far] * len(raw),
            out_specs=(vmem,) * len(shapes),
            scratch_shapes=[pltpu.VMEM(w.shape, BF) for w in raw]
            + [
                pltpu.VMEM((4, 4 * n1, 4 * n1), BF),
                pltpu.VMEM((2, 4 * n1, 128), BF),
                pltpu.VMEM((128, 4 * n1), F32),
                pltpu.VMEM((2 * n1, 2 * n1), F32),
                pltpu.SemaphoreType.DMA((len(raw),)),
            ],
            compiler_params=pltpu.CompilerParams(vmem_limit_bytes=63 * 2**20),
            cost_estimate=pl.CostEstimate(
                flops=10**9, bytes_accessed=10**7, transcendentals=0
            ),
            name="lay",
        )(*raw)
        if planes == 1:
            others = tile[None]
        elif planes == 2:
            others = lax.ppermute(tile, "plane", [(0, 1), (1, 0)])[None]
        else:
            ahead = [(i, i + 1) for i in range(planes - 1)]
            behind = [(i + 1, i) for i in range(planes - 1)]
            others = jnp.stack(
                [lax.ppermute(tile, "plane", ahead), lax.ppermute(tile, "plane", behind)]
            )
        constants = [jnp.asarray(m) for m in unpack_constants(z)]
        w_pf = pool_fine.transpose(0, 2, 1).reshape(4 * n1, n2)
        operands = [
            noisy, *constants[:4], bias, weights[0], w_pf, *weights[1:],
            *constants[4:],
        ]
        cells = z.cells
        return pl.pallas_call(
            lambda *refs: net_kernel(z, len(operands), *refs),
            out_shape=(
                jax.ShapeDtypeStruct(noisy.shape, BF),
                jax.ShapeDtypeStruct(noisy.shape, F32),
            ),
            in_specs=[smem, vmem, vmem] + [far] * len(operands),
            out_specs=(far, far),
            scratch_shapes=[pltpu.VMEM(w.shape, w.dtype) for w in operands]
            + [
                pltpu.VMEM(noisy.shape, BF),
                pltpu.VMEM(noisy.shape, F32),
                pltpu.VMEM((z.ext, cols + 128), BF),
                pltpu.VMEM((z.gi * 40, 384), F32),
                pltpu.VMEM((cells, 256), BF),
                pltpu.VMEM((4, cells, 4 * n1), BF),
                pltpu.VMEM((cells, 4 * n2), BF),
                pltpu.VMEM((cells, n3), BF),
                pltpu.VMEM((cells, z.slots * inner), BF),
                pltpu.VMEM((cells, 3 * n3), BF),
                pltpu.VMEM((2, cells, 4 * n2), BF),
                pltpu.VMEM((4, cells, 6 * n1), BF),
                pltpu.VMEM((4, cells, 6 * n1), BF),
                pltpu.VMEM((rows // 4 * 24, 2 * z.step), F32),
                pltpu.VMEM((cells, 128), F32),
                pltpu.VMEM((cells, 128), F32),
                pltpu.VMEM((cells, 128), F32),
                pltpu.SemaphoreType.DMA((len(operands),)),
                pltpu.SemaphoreType.DMA((2,)),
            ],
            compiler_params=pltpu.CompilerParams(vmem_limit_bytes=63 * 2**20),
            name="net",
        )(owner, recv, others, *operands)

    copied = P()
    in_specs = (
        P("plane", None, "height", "span"),
        P(AXES, None, None, None, None),
    ) + (copied,) * 15
    out_specs = (P("plane", None, "height", "span"), P("plane", None, "height", "span"))
    return jax.shard_map(shards, mesh=mesh, in_specs=in_specs, out_specs=out_specs, check_vma=False)
```

```python
import math

import jax
import jax.numpy as jnp
import numpy as np
from jax import lax
from jax.experimental import pallas as pl
from jax.experimental.pallas import tpu as pltpu
from jax.sharding import PartitionSpec as P

CF = 8
TSTEPS = 1000
STRIDE = 20
RIM = 9
EDGE = 2
BF = jnp.bfloat16
F32 = jnp.float32
AXES = ("plane", "span", "height")


def up(n, m):
    return -(-n // m) * m


def dot(a, b):
    return jnp.dot(a, b, preferred_element_type=F32)


def dot_nt(a, b):
    return lax.dot_general(a, b, (((1,), (1,)), ((), ())), preferred_element_type=F32)


def silu(x):
    half = 0.5 * x
    return half + half * jnp.tanh(half)


class Sizes:
    def __init__(self, rows, cols, planes, spans, heights, cond_rows, cond_cols):
        self.rows, self.cols = rows, cols
        self.planes, self.spans, self.heights = planes, spans, heights
        self.cond_rows, self.cond_cols = cond_rows, cond_cols
        self.devices = planes * spans * heights
        self.gi, self.gj = rows // 4 + 2 * EDGE, cols // 4 + 2 * EDGE
        self.step = up(self.gj, 8)
        self.cells = self.gi * self.step
        self.slots = min(planes, 3)
        self.strip = up(3 * RIM, 16)
        self.ext = 2 * self.strip + 3 * rows
        self.patch_rows, self.patch_cols = rows // CF + 4, cols // CF + 4
        self.pairs = (self.slots + 1) // 2
        self.piece = up(3 * RIM + self.patch_rows * self.pairs, 8)
        self.pad = up(3 * RIM + self.patch_rows * self.pairs, 8)
        self.patch = up(self.piece, 16)

    def planes_of(self, plane):
        if self.planes == 1:
            return [plane]
        if self.planes == 2:
            return [plane, 1 - plane]
        return [plane, plane - 1, plane + 1]


def unpack_constants(z):
    across = np.zeros((z.cols + 128, 6 * 64), np.float32)
    lift = np.zeros((2, 3, 128, 6 * 64), np.float32)
    for b in range(6):
        for j in range(z.gj):
            col = 4 * (j - EDGE) - 1 + b
            if col < 0:
                across[z.cols + 128 + col, b * 64 + j] = 1
            elif col < z.cols:
                across[col, b * 64 + j] = 1
            else:
                across[z.cols + col - z.cols, b * 64 + j] = 1
            for half in range(2):
                for c in range(3):
                    lift[half, c, half * 64 + c * z.patch_cols + col // CF + 2, b * 64 + j] = 1
    down = np.zeros((z.pairs, z.gi * 40, z.ext + 3 * z.patch), np.float32)
    for i in range(z.gi):
        for c in range(3):
            for a in range(6):
                row = 4 * (i - EDGE) - 1 + a
                if row < 0:
                    source = c * RIM + row + RIM
                elif row < z.rows:
                    source = z.strip + c * z.rows + row
                else:
                    source = z.strip + 3 * z.rows + c * RIM + row - z.rows
                down[:, i * 40 + c * 6 + a, source] = 1
                for pair in range(z.pairs):
                    at = z.ext + c * z.patch + 3 * RIM + pair * z.patch_rows + row // CF + 2
                    down[pair, i * 40 + 18 + c * 6 + a, at] = 1
    sides = np.zeros((2 * 16, 128), np.float32)
    for r in range(RIM):
        sides[r, 128 - RIM + r] = 1
        sides[16 + r, r] = 1
    spread = np.zeros((2 * z.step, 2 * z.cols), np.float32)
    for pair in range(2):
        for j in range(z.cols // 4):
            for b in range(2):
                spread[pair * z.step + j + EDGE, b * z.cols + 4 * j + 2 * pair + b] = 1
    inner = z.rows // 4
    gather = np.zeros((2, 3 * z.rows, inner * 24), np.float32)
    for b in range(2):
        for i in range(inner):
            for a in range(4):
                for o in range(3):
                    gather[b, o * z.rows + 4 * i + a, i * 24 + a * 6 + b * 3 + o] = 1
    return tuple(
        m.astype(BF) for m in (sides, across, lift.reshape(-1, 6 * 64), down, spread, gather)
    )


def fetch(pairs, sems):
    copies = [
        pltpu.make_async_copy(source, target, sems.at[n])
        for n, (source, target) in enumerate(pairs)
    ]
    for copy in copies:
        copy.start()
    return copies


def pack_kernel(z, noisy_hbm, slot_hbm, send, noisy, slot, padded, sems):
    tile_copy, slot_copy = fetch(((noisy_hbm, noisy), (slot_hbm, slot)), sems)
    plane, span, height = (lax.axis_index(a) for a in AXES)
    tall, across = z.rows // CF, z.cols // CF

    shape = (z.cond_cols, z.spans * 128)
    col = lax.broadcasted_iota(jnp.int32, shape, 0)
    lane = lax.broadcasted_iota(jnp.int32, shape, 1)
    windows = []
    for c in range(3):
        x = (lane & 127) - c * z.patch_cols
        hit = (x >= 0) & (x < z.patch_cols) & (col == (lane >> 7) * across + x - 2)
        windows.append(jnp.where(hit, 1.0, 0.0).astype(BF))
    shape = (2 * z.strip, 3 * z.rows)
    row = lax.broadcasted_iota(jnp.int32, shape, 0)
    lane = lax.broadcasted_iota(jnp.int32, shape, 1)
    strips = jnp.zeros(shape, F32)
    for half, first in ((0, z.rows - RIM), (z.strip, 0)):
        for c in range(3):
            r = row - half - c * RIM
            hit = (r >= 0) & (r < RIM) & (lane == c * z.rows + first + r)
            strips = jnp.where(hit, 1.0, strips)
    strips = strips.astype(BF)
    shape = (32, z.cols)
    row = lax.broadcasted_iota(jnp.int32, shape, 0)
    lane = lax.broadcasted_iota(jnp.int32, shape, 1)
    hit = (row < RIM) & (lane == z.cols - RIM + row)
    hit = hit | ((row >= 16) & (row < 16 + RIM) & (lane == row - 16))
    sides = jnp.where(hit, 1.0, 0.0).astype(BF)

    base = 3 * RIM
    padded[...] = jnp.zeros_like(padded)
    slot_copy.wait()
    wide = None
    for c in range(3):
        part = dot(slot[0, :, c].reshape(z.planes * z.cond_rows, z.cond_cols), windows[c])
        wide = part if wide is None else wide + part
    for p in range(z.planes):
        at = z.pad + 2
        padded[p, at : at + z.cond_rows, :] = wide[p * z.cond_rows : (p + 1) * z.cond_rows]
    tile_copy.wait()
    tile = noisy[0].reshape(3 * z.rows, z.cols)
    ends = dot(strips, tile)
    cols = dot_nt(sides, tile)

    rows = lax.broadcasted_iota(jnp.int32, (z.piece, 128), 0)
    for p in range(z.planes):
        for s in range(z.spans):
            for h in range(z.heights):
                target = (p * z.spans + s) * z.heights + h
                total = jnp.zeros((z.piece, 128), F32)
                for k0 in range(0, z.slots, 2):
                    first = base + k0 // 2 * z.patch_rows
                    mine = (rows >= first) & (rows < first + z.patch_rows)
                    both = None
                    for k in range(k0, min(k0 + 2, z.slots)):
                        q = z.planes_of(p)[k]
                        if 0 <= q < z.planes:
                            at = z.pad + tall * h - first
                            part = padded[q, at : at + z.piece, s * 128 : (s + 1) * 128]
                            part = part if k == k0 else pltpu.roll(part, 64, 1)
                            both = part if both is None else both + part
                    if both is not None:
                        total = jnp.where(mine, both, total)
                send[target] = total.astype(BF)
    rest = jnp.zeros((z.piece - z.strip, 128), F32)
    blank = jnp.zeros((16, 128 - (3 * z.rows) % 128), F32)
    side = []
    for half in (0, 16):
        part = jnp.concatenate([cols[half : half + 16], blank], axis=1)
        side.append(
            jnp.concatenate([part[:, 0:128], part[:, 128:256], rest], axis=0)
        )
    ends = [
        jnp.concatenate([ends[half : half + z.strip], rest], axis=0) for half in (0, z.strip)
    ]
    for k in range(z.slots):
        q = z.planes_of(plane)[k]
        for dh in (-1, 0, 1):
            for ds in (-1, 0, 1):
                if dh == 0 and ds == 0:
                    continue
                ok = (
                    (q >= 0) & (q < z.planes)
                    & (span + ds >= 0) & (span + ds < z.spans)
                    & (height + dh >= 0) & (height + dh < z.heights)
                )

                @pl.when(ok)
                def _(q=q, dh=dh, ds=ds):
                    target = (q * z.spans + span + ds) * z.heights + height + dh
                    if dh != 0:
                        strip = ends[0 if dh > 0 else 1]
                    else:
                        strip = side[0 if ds > 0 else 1]
                    send[target] = (send[target].astype(F32) + strip).astype(BF)


def net_kernel(
    z, count, owner, *refs
):
    far, refs = refs[:count], refs[count:]
    pred_far, sample_far, refs = refs[0], refs[1], refs[2:]
    near, refs = refs[:count], refs[count:]
    (pred, sample, ext, grid, entry, h1, d1, d2, sq, mx, v2, v1, e1, last,
     mask, half, halfp, sems, out_sems) = refs
    copies = fetch(tuple(zip(far, near)), sems)
    recv, others, noisy, sides, across, lift, down, bias = near[:8]
    w_in, w_pf, w_pm, w_sq, w_ac, w_mid, w_rm, w_dm, w_rf, w_df, w_lv, spread, gather = near[8:]
    plane, span, height = (lax.axis_index(a) for a in AXES)
    step, gi = z.step, z.gi
    n1, n2, n3 = w_in.shape[1] // 16, w_pf.shape[1], w_pm.shape[1]
    inner = z.rows // 4

    shape = (gi, step, 128)
    row = lax.broadcasted_iota(jnp.int32, shape, 0) + (height * inner - EDGE)
    col = lax.broadcasted_iota(jnp.int32, shape, 1) + (span * (z.cols // 4) - EDGE)
    lane = lax.broadcasted_iota(jnp.int32, shape, 2)
    row_in = (row >= 0) & (row < z.heights * inner)
    wide = z.spans * (z.cols // 4)
    here = row_in & (col >= 0) & (col < wide)
    colp = col + jnp.where(lane >= n1, 1, 0)
    herep = row_in & (colp >= 0) & (colp < wide)
    mask[...] = jnp.where(here, 1.0, 0.0).reshape(z.cells, 128)
    half[...] = jnp.where(here, 0.5, 0.0).reshape(z.cells, 128)
    halfp[...] = jnp.where(herep, 0.5, 0.0).reshape(z.cells, 128)

    def masked(x, rows, ref=mask):
        m = ref[rows, :]
        return x * jnp.concatenate([m] * (x.shape[1] // 128), axis=1)

    lanes = lax.broadcasted_iota(jnp.int32, (z.strip, 128), 1)
    for copy in copies[:7]:
        copy.wait()
    for k in range(z.slots):
        q = z.planes_of(plane)[k]

        def piece(dh, ds, q=q):
            ok = (
                (q >= 0) & (q < z.planes)
                & (span + ds >= 0) & (span + ds < z.spans)
                & (height + dh >= 0) & (height + dh < z.heights)
            )
            source = (q * z.spans + span + ds) * z.heights + height + dh
            source = jnp.clip(source, 0, z.devices - 1)
            value = recv[source].astype(F32)[0 : z.strip]
            return jnp.where(ok, value, 0.0)

        tile = (noisy[0] if k == 0 else others[k - 1]).reshape(3 * z.rows, z.cols)
        ext[z.strip : z.strip + 3 * z.rows, 0 : z.cols] = tile
        for dh, base in ((-1, 0), (1, z.strip + 3 * z.rows)):
            ext[base : base + z.strip, 0 : z.cols] = piece(dh, 0).astype(BF)
            left, right = piece(dh, -1), piece(dh, 1)
            rim = jnp.where(lanes >= 128 - RIM, left, jnp.where(lanes < RIM, right, 0.0))
            ext[base : base + z.strip, z.cols : z.cols + 128] = rim.astype(BF)
        left, right = piece(0, -1), piece(0, 1)
        halves = [
            jnp.concatenate([v[0:16], v[16:32]], axis=1) for v in (left, right)
        ]
        rims = jnp.concatenate(halves, axis=0)
        rims = jnp.transpose(rims)[0 : 3 * z.rows].astype(BF)
        ext[z.strip : z.strip + 3 * z.rows, z.cols : z.cols + 128] = dot(
            rims, sides[...]
        ).astype(BF)
        patch = recv[owner[0]].astype(F32)
        patch = jnp.concatenate([patch, jnp.zeros((z.patch - z.piece, 128), F32)], axis=0)
        patch = patch.astype(BF)
        wide_rows = [dot(ext[...], across[...]).astype(BF)]
        for c in range(3):
            at = (k % 2 * 3 + c) * 128
            wide_rows.append(dot(patch, lift[at : at + 128, :]).astype(BF))
        grid[...] = dot(down[k // 2], jnp.concatenate(wide_rows, axis=0))
        for i in range(gi):
            block = grid[i * 40 : (i + 1) * 40, :]
            stack = jnp.concatenate(
                [block[:, 0:128], block[:, 128:256], block[:, 256:384], jnp.zeros((8, 128), F32)],
                axis=0,
            )
            turned = jnp.transpose(stack)
            at = i * step
            entry[at : at + step, 0:128] = turned[0:step]
            entry[at : at + step, 128:256] = turned[64 : 64 + step]
        if k == 0:
            for copy in copies[7:12]:
                copy.wait()
            b1 = bias[:, 0:n1]
            b1 = jnp.concatenate([b1] * 4, axis=1)
            b2 = bias[:, n1 : n1 + n2]
            b3 = bias[:, n1 + n2 : n1 + n2 + n3]
        per = gi
        for i in range(0, gi, per):
            rows = slice(i * step, (i + per) * step)
            x = entry[rows, :].astype(BF)
            mids = []
            for g in range(4):
                h = dot(x, w_in[:, g * 4 * n1 : (g + 1) * 4 * n1]) + b1
                h = silu(h).astype(BF)
                if k == 0:
                    h1[g, rows, :] = h
                m = silu(dot(h, w_pf[...]) + b2).astype(BF)
                if k == 0:
                    d1[rows, g * n2 : (g + 1) * n2] = m
                mids.append(m)
            low = silu(dot(jnp.concatenate(mids, axis=1), w_pm[...]) + b3).astype(BF)
            if k == 0:
                d2[rows, :] = low
            width = w_sq.shape[1]
            sq[rows, k * width : (k + 1) * width] = dot(low, w_sq[...]).astype(BF)

    def rows_of(first, last_):
        return slice(first * step // 16 * 16, up(last_ * step, 16))

    def above(x):
        return jnp.concatenate([x[-step:], x[:-step]], axis=0)

    def below(x):
        return jnp.concatenate([x[step:], x[:step]], axis=0)

    for copy in copies[12:]:
        copy.wait()
    m = d2[...].astype(F32) + dot(sq[...], w_ac[...])
    m = masked(m, slice(0, z.cells))
    for a, ma in enumerate((above(m), m, below(m))):
        at = 3 * n3 * a
        mx[:, at + n3 : at + 2 * n3] = ma.astype(BF)
    for b, mb in enumerate((pltpu.roll(m, 1, 0), pltpu.roll(m, z.cells - 1, 0))):
        for a, ma in enumerate((above(mb), mb, below(mb))):
            at = 3 * n3 * a + 2 * b * n3
            mx[:, at : at + n3] = ma.astype(BF)

    rows = rows_of(1, gi - 1)
    n = rows.stop - rows.start
    c = silu(dot(mx[rows, :], w_mid[...])).astype(BF)
    v = dot(c, w_rm[...]) + d1[rows, :].astype(F32)
    v = masked(v, rows)
    for p in range(2):
        vp = v[:, 2 * p * n2 : 2 * (p + 1) * n2]
        left = pltpu.roll(vp[:, n2:], 1, 0)
        right = pltpu.roll(vp[:, :n2], n - 1, 0)
        turn = below if p == 0 else above
        for at, part in ((n2, vp), (0, left), (3 * n2, right)):
            v2[p, rows, at : at + part.shape[1]] = part.astype(BF)
            v2[3 - p, rows, at : at + part.shape[1]] = turn(part).astype(BF)

    for p in range(2):
        rows = rows_of(1, gi - 1 - p)
        n = rows.stop - rows.start
        wide = [v2[at, rows, :] for at in ((2, 0, 1), (0, 1, 3))[p]]
        e = silu(dot(jnp.concatenate(wide, axis=1), w_dm[...])).astype(BF)
        for q in range(2):
            v = dot(e[:, q * n2 : (q + 1) * n2], w_rf[...])
            v = masked(v + h1[2 * p + q, rows, :].astype(F32), rows)
            for a in range(2):
                va = v[:, 2 * a * n1 : 2 * (a + 1) * n1]
                parts = [(2 * q * n1, va)]
                if q == 0:
                    parts.append((4 * n1, pltpu.roll(va, n - 1, 0)))
                for at, part in parts:
                    v1[2 * p + a, rows, at : at + 2 * n1] = part.astype(BF)
                    if p == 0:
                        v1[4 + a, rows, at : at + 2 * n1] = below(part).astype(BF)

    for turn in range(2):
        rows = rows_of(2 - turn, gi - 2)
        n = rows.stop - rows.start
        for pair in range(2):
            lanes_in = slice(2 * pair * n1, (2 * pair + 4) * n1)
            wide = [v1[at, rows, lanes_in] for at in ((0, 1, 2, 3), (2, 3, 4, 5))[turn]]
            x = dot(jnp.concatenate(wide, axis=1), w_df[...])
            for a in range(2):
                shift = step if turn and a else 0
                there = slice(rows.start + shift, rows.stop + shift)
                t = masked(
                    x[:, 2 * a * n1 : 2 * (a + 1) * n1], there, halfp if pair else half
                )
                t = t + t * jnp.tanh(t)
                parts = [((2 + 2 * pair) * n1, t)]
                if pair == 1:
                    parts.append((0, pltpu.roll(t, 1, 0)))
                for at, part in parts:
                    e1[2 * turn + a, rows, at : at + 2 * n1] = part.astype(BF)
                    if turn:
                        e1[4 + a, rows, at : at + 2 * n1] = above(part).astype(BF)

    rows = rows_of(2, gi - 2)
    outs = []
    for pair in range(2):
        lanes_in = slice(2 * pair * n1, (2 * pair + 4) * n1)
        wide = [e1[at, rows, lanes_in] for at in (4, 5, 0, 1, 2, 3)]
        outs.append(dot(jnp.concatenate(wide, axis=1), w_lv[...]))
    for r in range(inner):
        at = (2 + r) * step - rows.start
        block = jnp.concatenate([o[at : at + step] for o in outs], axis=0)
        last[r * 24 : (r + 1) * 24, :] = jnp.transpose(block)[0:24]
    spread_out = dot(last[...].astype(BF), spread[...]).astype(BF)
    guess = dot(gather[0], spread_out[:, 0 : z.cols])
    guess = guess + dot(gather[1], spread_out[:, z.cols :])
    pred[0] = guess.astype(BF).reshape(3, z.rows, z.cols)
    pred_copy = pltpu.make_async_copy(pred, pred_far, out_sems.at[0])
    pred_copy.start()
    given = noisy[0].reshape(3 * z.rows, z.cols).astype(F32)
    at = n1 + n2 + n3
    back, rise, keep, add = (bias[:, at + t : at + t + 1] for t in range(4))
    result = keep * ((given - back * guess) * rise) + add * guess
    sample[0] = result.reshape(3, z.rows, z.cols)
    sample_copy = pltpu.make_async_copy(sample, sample_far, out_sems.at[1])
    sample_copy.start()
    pred_copy.wait()
    sample_copy.wait()


def plan(stepnum):
    phase = (stepnum.astype(F32) / TSTEPS + 0.008) / 1.008 * (math.pi / 2.0)
    return jnp.cos(phase) ** 2


def time_bias(timestep, w_embed, w_biases):
    half = w_embed.shape[0] // 2
    freqs = jnp.exp(-math.log(10000.0) * jnp.arange(half, dtype=F32) / half)
    angles = timestep[0].astype(F32) * freqs
    waves = jnp.concatenate([jnp.sin(angles), jnp.cos(angles)])
    hidden = jax.nn.silu(jnp.dot(waves, w_embed, precision=lax.Precision.HIGHEST))
    return jnp.dot(hidden, w_biases, precision=lax.Precision.HIGHEST)


def entry_constants():
    place = np.zeros((8, 256, 128), np.float32)
    for y in range(4):
        for pair in range(2):
            for h in range(2):
                for la in range(3):
                    for lb in range(3):
                        for cin in range(6):
                            a, b = y + la, 2 * pair + h + lb
                            row = b % 2 * 128 + b // 2 * 40 + cin * 6 + a
                            place[y * 2 + pair, row, h * 64 + la * 18 + lb * 6 + cin] = 1
    return place.astype(BF)


def lay_kernel(z, count, *refs):
    far, refs = refs[:count], refs[count:]
    tile, refs = refs[0], refs[1:]
    w_in, w_pm, w_sq, w_ac, w_mid, w_rm, w_dm, w_rf, w_df, w_lv = refs[:10]
    near, refs = refs[10 : 10 + count], refs[10 + count :]
    nat, tall, leave, enter, sems = refs
    copies = fetch(tuple(zip(far, near)), sems)
    (noisy, place, w_enter, w_leave, pool_mid, w_squeeze, w_across, w_middle,
     rise_mid, decode_mid, rise_fine, decode_fine) = near
    plane = lax.axis_index("plane")
    n1, n2, n3 = decode_fine.shape[1], decode_mid.shape[1], w_middle.shape[1]

    for copy in copies:
        copy.wait()
    tile[...] = noisy[0]
    tall[...] = jnp.zeros_like(tall)
    leave[...] = jnp.zeros_like(leave)
    enter[...] = jnp.zeros_like(enter)
    blank = jnp.zeros(w_enter.shape[1:], F32)
    for a in range(3):
        leave[3 * a : 3 * a + 3, 0 : 3 * n1] = w_leave[a].astype(F32)
        for h in range(2):
            taps = w_enter[a].astype(F32)
            taps = jnp.concatenate([blank, taps] if h else [taps, blank], axis=1)
            enter[h * n1 + a * 18 : h * n1 + a * 18 + 18, :] = taps
    turned = jnp.transpose(leave[...])[0 : 3 * n1].astype(BF)
    spots = enter[...].astype(BF)
    for b in range(2):
        tall[b, b * n1 : (b + 3) * n1, :] = turned
    line = lax.broadcasted_iota(jnp.int32, (128, 128), 0)
    lane = lax.broadcasted_iota(jnp.int32, (128, 128), 1)
    for y in range(6):
        total = None
        for b in range(2):
            pick = jnp.zeros((128, 128), F32)
            for a in range(4):
                if 0 <= y - a < 3:
                    o = lane - (6 * a + 3 * b)
                    hit = (o >= 0) & (o < 3) & (line == 3 * (y - a) + o)
                    pick = jnp.where(hit, 1.0, pick)
            part = dot(tall[b], pick.astype(BF))
            total = part if total is None else total + part
        w_lv[y * 4 * n1 : (y + 1) * 4 * n1, :] = total.astype(BF)

    for y in range(4):
        for pair in range(2):
            at = ((y // 2 * 2 + pair) * 2 + y % 2) * 2 * n1
            w_in[:, at : at + 2 * n1] = dot(place[y * 2 + pair], spots).astype(BF)
    for t in range(4):
        w_pm[t * n2 : (t + 1) * n2, :] = jnp.transpose(pool_mid[t])
        w_rm[:, t * n2 : (t + 1) * n2] = jnp.transpose(rise_mid[t])
    w_sq[...] = jnp.transpose(w_squeeze[...])
    width = w_across.shape[2]
    taps = [w_across[1]]
    zero = jnp.zeros_like(taps[0])
    if z.planes == 2:
        taps.append(jnp.where(plane == 0, w_across[2], w_across[0]))
    elif z.planes > 2:
        taps.append(jnp.where(plane > 0, w_across[0], zero))
        taps.append(jnp.where(plane < z.planes - 1, w_across[2], zero))
    for k, tap in enumerate(taps):
        w_ac[k * width : (k + 1) * width, :] = jnp.transpose(tap)
    for a in range(3):
        w_mid[a * 3 * n3 : (a + 1) * 3 * n3, :] = jnp.transpose(w_middle[a])
        turned = jnp.transpose(decode_mid[a])
        at = a * 4 * n2
        w_dm[at : at + 4 * n2, :] = jnp.zeros((4 * n2, 2 * n2), BF)
        w_dm[at : at + 3 * n2, 0:n2] = turned
        w_dm[at + n2 : at + 4 * n2, n2 : 2 * n2] = turned
    w_rf[...] = jnp.transpose(rise_fine[...].reshape(4 * n1, n2))

    nat[...] = jnp.zeros_like(nat)
    for a in range(3):
        for b in range(2):
            wide = jnp.concatenate(
                [decode_fine[a].astype(F32), jnp.zeros((n1, n1), F32)], axis=1
            )
            wide = pltpu.roll(wide, b * n1, 1) if b else wide
            for r in range(2):
                nat[a + r, (2 * r + b) * n1 : (2 * r + b + 1) * n1, :] = wide.astype(BF)
    for a in range(4):
        w_df[a * 4 * n1 : (a + 1) * 4 * n1, :] = jnp.transpose(nat[a])


def solution(mesh):
    planes, spans, heights = (mesh.shape[a] for a in AXES)

    def shards(
        noisy, coarse_cond, timestep, owner, w_embed, w_biases, w_enter, pool_fine, pool_mid,
        w_squeeze, w_across, w_middle, rise_mid, decode_mid, rise_fine, decode_fine, w_leave,
    ):
        rows, cols = noisy.shape[2:]
        z = Sizes(rows, cols, planes, spans, heights, *coarse_cond.shape[3:])
        n1, n2, n3 = w_enter.shape[1], pool_fine.shape[1], pool_mid.shape[1]
        vmem = pl.BlockSpec(memory_space=pltpu.VMEM)
        smem = pl.BlockSpec(memory_space=pltpu.SMEM)
        far = pl.BlockSpec(memory_space=pltpu.HBM)
        send = pl.pallas_call(
            lambda *refs: pack_kernel(z, *refs),
            out_shape=jax.ShapeDtypeStruct((z.devices, z.piece, 128), BF),
            in_specs=[far] * 2,
            out_specs=vmem,
            scratch_shapes=[
                pltpu.VMEM(noisy.shape, BF),
                pltpu.VMEM(coarse_cond.shape, BF),
                pltpu.VMEM((planes, up(z.cond_rows, 8) + 2 * z.pad, spans * 128), F32),
                pltpu.SemaphoreType.DMA((2,)),
            ],
            compiler_params=pltpu.CompilerParams(vmem_limit_bytes=63 * 2**20),
            name="pack",
        )(noisy, coarse_cond)
        recv = lax.all_to_all(send, AXES, 0, 0, tiled=True)
        now, prior = plan(timestep[0]), plan(timestep[0] - STRIDE)
        coefs = jnp.stack(
            [jnp.sqrt(1.0 - now), 1.0 / jnp.sqrt(now), jnp.sqrt(prior), jnp.sqrt(1.0 - prior)]
        )
        bias = jnp.concatenate([time_bias(timestep, w_embed, w_biases), coefs])[None]
        raw = (
            noisy, jnp.asarray(entry_constants()), w_enter.transpose(0, 2, 1), w_leave, pool_mid,
            w_squeeze, w_across, w_middle, rise_mid, decode_mid, rise_fine, decode_fine,
        )
        inner = w_squeeze.shape[0]
        shapes = (
            noisy.shape[1:],
            (256, 16 * n1), (4 * n2, n3), (n3, inner), (z.slots * inner, n3),
            (9 * n3, n3), (n3, 4 * n2), (12 * n2, 2 * n2), (n2, 4 * n1),
            (16 * n1, 4 * n1), (24 * n1, 128),
        )
        tile, *weights = pl.pallas_call(
            lambda *refs: lay_kernel(z, len(raw), *refs),
            out_shape=tuple(jax.ShapeDtypeStruct(shape, BF) for shape in shapes),
            in_specs=[far] * len(raw),
            out_specs=(vmem,) * len(shapes),
            scratch_shapes=[pltpu.VMEM(w.shape, BF) for w in raw]
            + [
                pltpu.VMEM((4, 4 * n1, 4 * n1), BF),
                pltpu.VMEM((2, 4 * n1, 128), BF),
                pltpu.VMEM((128, 4 * n1), F32),
                pltpu.VMEM((2 * n1, 2 * n1), F32),
                pltpu.SemaphoreType.DMA((len(raw),)),
            ],
            compiler_params=pltpu.CompilerParams(vmem_limit_bytes=63 * 2**20),
            cost_estimate=pl.CostEstimate(
                flops=10**9, bytes_accessed=10**7, transcendentals=0
            ),
            name="lay",
        )(*raw)
        if planes == 1:
            others = tile[None]
        elif planes == 2:
            others = lax.ppermute(tile, "plane", [(0, 1), (1, 0)])[None]
        else:
            ahead = [(i, i + 1) for i in range(planes - 1)]
            behind = [(i + 1, i) for i in range(planes - 1)]
            others = jnp.stack(
                [lax.ppermute(tile, "plane", ahead), lax.ppermute(tile, "plane", behind)]
            )
        constants = [jnp.asarray(m) for m in unpack_constants(z)]
        w_pf = pool_fine.transpose(0, 2, 1).reshape(4 * n1, n2)
        operands = [
            recv, others, noisy, *constants[:4], bias, weights[0], w_pf, *weights[1:],
            *constants[4:],
        ]
        cells = z.cells
        return pl.pallas_call(
            lambda *refs: net_kernel(z, len(operands), *refs),
            out_shape=(
                jax.ShapeDtypeStruct(noisy.shape, BF),
                jax.ShapeDtypeStruct(noisy.shape, F32),
            ),
            in_specs=[smem] + [far] * len(operands),
            out_specs=(far, far),
            scratch_shapes=[pltpu.VMEM(w.shape, w.dtype) for w in operands]
            + [
                pltpu.VMEM(noisy.shape, BF),
                pltpu.VMEM(noisy.shape, F32),
                pltpu.VMEM((z.ext, cols + 128), BF),
                pltpu.VMEM((z.gi * 40, 384), F32),
                pltpu.VMEM((cells, 256), F32),
                pltpu.VMEM((4, cells, 4 * n1), BF),
                pltpu.VMEM((cells, 4 * n2), BF),
                pltpu.VMEM((cells, n3), BF),
                pltpu.VMEM((cells, z.slots * inner), BF),
                pltpu.VMEM((cells, 9 * n3), BF),
                pltpu.VMEM((4, cells, 4 * n2), BF),
                pltpu.VMEM((6, cells, 6 * n1), BF),
                pltpu.VMEM((6, cells, 6 * n1), BF),
                pltpu.VMEM((rows // 4 * 24, 2 * z.step), F32),
                pltpu.VMEM((cells, 128), F32),
                pltpu.VMEM((cells, 128), F32),
                pltpu.VMEM((cells, 128), F32),
                pltpu.SemaphoreType.DMA((len(operands),)),
                pltpu.SemaphoreType.DMA((2,)),
            ],
            compiler_params=pltpu.CompilerParams(vmem_limit_bytes=63 * 2**20),
            name="net",
        )(owner, *operands)

    copied = P()
    in_specs = (
        P("plane", None, "height", "span"),
        P(AXES, None, None, None, None),
    ) + (copied,) * 15
    out_specs = (P("plane", None, "height", "span"), P("plane", None, "height", "span"))
    return jax.shard_map(shards, mesh=mesh, in_specs=in_specs, out_specs=out_specs, check_vma=False)
```

```python
import math

import jax
import jax.numpy as jnp
import numpy as np
from jax import lax
from jax.experimental import pallas as pl
from jax.experimental.pallas import tpu as pltpu
from jax.sharding import PartitionSpec as P

CF = 8
TSTEPS = 1000
STRIDE = 20
RIM = 9
EDGE = 2
BF = jnp.bfloat16
F32 = jnp.float32
AXES = ("plane", "span", "height")


def up(n, m):
    return -(-n // m) * m


def dot(a, b):
    return jnp.dot(a, b, preferred_element_type=F32)


def dot_nt(a, b):
    return lax.dot_general(a, b, (((1,), (1,)), ((), ())), preferred_element_type=F32)


def silu(x):
    half = 0.5 * x
    return half + half * jnp.tanh(half)


class Sizes:
    def __init__(self, rows, cols, planes, spans, heights, cond_rows, cond_cols):
        self.rows, self.cols = rows, cols
        self.planes, self.spans, self.heights = planes, spans, heights
        self.cond_rows, self.cond_cols = cond_rows, cond_cols
        self.devices = planes * spans * heights
        self.gi, self.gj = rows // 4 + 2 * EDGE, cols // 4 + 2 * EDGE
        self.step = up(self.gj, 8)
        self.cells = self.gi * self.step
        self.slots = min(planes, 3)
        self.strip = up(3 * RIM, 16)
        self.ext = 2 * self.strip + 3 * rows
        self.patch_rows, self.patch_cols = rows // CF + 4, cols // CF + 4
        self.pairs = (self.slots + 1) // 2
        self.piece = up(3 * RIM + self.patch_rows * self.pairs, 8)
        self.pad = up(3 * RIM + self.patch_rows * self.pairs, 8)
        self.patch = up(self.piece, 16)

    def planes_of(self, plane):
        if self.planes == 1:
            return [plane]
        if self.planes == 2:
            return [plane, 1 - plane]
        return [plane, plane - 1, plane + 1]


def unpack_constants(z):
    across = np.zeros((z.cols + 128, 6 * 64), np.float32)
    lift = np.zeros((2, 3, 128, 6 * 64), np.float32)
    for b in range(6):
        for j in range(z.gj):
            col = 4 * (j - EDGE) - 1 + b
            if col < 0:
                across[z.cols + 128 + col, b * 64 + j] = 1
            elif col < z.cols:
                across[col, b * 64 + j] = 1
            else:
                across[z.cols + col - z.cols, b * 64 + j] = 1
            for half in range(2):
                for c in range(3):
                    lift[half, c, half * 64 + c * z.patch_cols + col // CF + 2, b * 64 + j] = 1
    down = np.zeros((z.pairs, z.gi * 40, z.ext + 3 * z.patch), np.float32)
    for i in range(z.gi):
        for c in range(3):
            for a in range(6):
                row = 4 * (i - EDGE) - 1 + a
                if row < 0:
                    source = c * RIM + row + RIM
                elif row < z.rows:
                    source = z.strip + c * z.rows + row
                else:
                    source = z.strip + 3 * z.rows + c * RIM + row - z.rows
                down[:, i * 40 + c * 6 + a, source] = 1
                for pair in range(z.pairs):
                    at = z.ext + c * z.patch + 3 * RIM + pair * z.patch_rows + row // CF + 2
                    down[pair, i * 40 + 18 + c * 6 + a, at] = 1
    sides = np.zeros((2 * 16, 128), np.float32)
    for r in range(RIM):
        sides[r, 128 - RIM + r] = 1
        sides[16 + r, r] = 1
    spread = np.zeros((2 * z.step, 2 * z.cols), np.float32)
    for pair in range(2):
        for j in range(z.cols // 4):
            for b in range(2):
                spread[pair * z.step + j + EDGE, b * z.cols + 4 * j + 2 * pair + b] = 1
    inner = z.rows // 4
    gather = np.zeros((2, 3 * z.rows, inner * 24), np.float32)
    for b in range(2):
        for i in range(inner):
            for a in range(4):
                for o in range(3):
                    gather[b, o * z.rows + 4 * i + a, i * 24 + a * 6 + b * 3 + o] = 1
    return tuple(
        m.astype(BF) for m in (sides, across, lift.reshape(-1, 6 * 64), down, spread, gather)
    )


def fetch(pairs, sems):
    copies = [
        pltpu.make_async_copy(source, target, sems.at[n])
        for n, (source, target) in enumerate(pairs)
    ]
    for copy in copies:
        copy.start()
    return copies


def pack_kernel(z, noisy_hbm, slot_hbm, send, noisy, slot, padded, sems):
    tile_copy, slot_copy = fetch(((noisy_hbm, noisy), (slot_hbm, slot)), sems)
    plane, span, height = (lax.axis_index(a) for a in AXES)
    tall, across = z.rows // CF, z.cols // CF

    shape = (z.cond_cols, z.spans * 128)
    col = lax.broadcasted_iota(jnp.int32, shape, 0)
    lane = lax.broadcasted_iota(jnp.int32, shape, 1)
    windows = []
    for c in range(3):
        x = (lane & 127) - c * z.patch_cols
        hit = (x >= 0) & (x < z.patch_cols) & (col == (lane >> 7) * across + x - 2)
        windows.append(jnp.where(hit, 1.0, 0.0).astype(BF))
    shape = (2 * z.strip, 3 * z.rows)
    row = lax.broadcasted_iota(jnp.int32, shape, 0)
    lane = lax.broadcasted_iota(jnp.int32, shape, 1)
    strips = jnp.zeros(shape, F32)
    for half, first in ((0, z.rows - RIM), (z.strip, 0)):
        for c in range(3):
            r = row - half - c * RIM
            hit = (r >= 0) & (r < RIM) & (lane == c * z.rows + first + r)
            strips = jnp.where(hit, 1.0, strips)
    strips = strips.astype(BF)
    shape = (32, z.cols)
    row = lax.broadcasted_iota(jnp.int32, shape, 0)
    lane = lax.broadcasted_iota(jnp.int32, shape, 1)
    hit = (row < RIM) & (lane == z.cols - RIM + row)
    hit = hit | ((row >= 16) & (row < 16 + RIM) & (lane == row - 16))
    sides = jnp.where(hit, 1.0, 0.0).astype(BF)

    base = 3 * RIM
    padded[...] = jnp.zeros_like(padded)
    slot_copy.wait()
    wide = None
    for c in range(3):
        part = dot(slot[0, :, c].reshape(z.planes * z.cond_rows, z.cond_cols), windows[c])
        wide = part if wide is None else wide + part
    for p in range(z.planes):
        at = z.pad + 2
        padded[p, at : at + z.cond_rows, :] = wide[p * z.cond_rows : (p + 1) * z.cond_rows]
    tile_copy.wait()
    tile = noisy[0].reshape(3 * z.rows, z.cols)
    ends = dot(strips, tile)
    cols = dot_nt(sides, tile)

    rows = lax.broadcasted_iota(jnp.int32, (z.piece, 128), 0)
    for p in range(z.planes):
        for s in range(z.spans):
            for h in range(z.heights):
                target = (p * z.spans + s) * z.heights + h
                total = jnp.zeros((z.piece, 128), F32)
                for k0 in range(0, z.slots, 2):
                    first = base + k0 // 2 * z.patch_rows
                    mine = (rows >= first) & (rows < first + z.patch_rows)
                    both = None
                    for k in range(k0, min(k0 + 2, z.slots)):
                        q = z.planes_of(p)[k]
                        if 0 <= q < z.planes:
                            at = z.pad + tall * h - first
                            part = padded[q, at : at + z.piece, s * 128 : (s + 1) * 128]
                            part = part if k == k0 else pltpu.roll(part, 64, 1)
                            both = part if both is None else both + part
                    if both is not None:
                        total = jnp.where(mine, both, total)
                send[target] = total.astype(BF)
    rest = jnp.zeros((z.piece - z.strip, 128), F32)
    blank = jnp.zeros((16, 128 - (3 * z.rows) % 128), F32)
    side = []
    for half in (0, 16):
        part = jnp.concatenate([cols[half : half + 16], blank], axis=1)
        side.append(
            jnp.concatenate([part[:, 0:128], part[:, 128:256], rest], axis=0)
        )
    ends = [
        jnp.concatenate([ends[half : half + z.strip], rest], axis=0) for half in (0, z.strip)
    ]
    for k in range(z.slots):
        q = z.planes_of(plane)[k]
        for dh in (-1, 0, 1):
            for ds in (-1, 0, 1):
                if dh == 0 and ds == 0:
                    continue
                ok = (
                    (q >= 0) & (q < z.planes)
                    & (span + ds >= 0) & (span + ds < z.spans)
                    & (height + dh >= 0) & (height + dh < z.heights)
                )

                @pl.when(ok)
                def _(q=q, dh=dh, ds=ds):
                    target = (q * z.spans + span + ds) * z.heights + height + dh
                    if dh != 0:
                        strip = ends[0 if dh > 0 else 1]
                    else:
                        strip = side[0 if ds > 0 else 1]
                    send[target] = (send[target].astype(F32) + strip).astype(BF)


def net_kernel(
    z, count, owner, *refs
):
    far, refs = refs[:count], refs[count:]
    pred_far, sample_far, refs = refs[0], refs[1], refs[2:]
    near, refs = refs[:count], refs[count:]
    (pred, sample, ext, grid, entry, h1, d1, d2, sq, mx, v2, v1, e1, last,
     mask, half, halfp, sems, out_sems) = refs
    copies = fetch(tuple(zip(far, near)), sems)
    recv, others, noisy, sides, across, lift, down, bias = near[:8]
    w_in, w_pf, w_pm, w_sq, w_ac, w_mid, w_rm, w_dm, w_rf, w_df, w_lv, spread, gather = near[8:]
    plane, span, height = (lax.axis_index(a) for a in AXES)
    step, gi = z.step, z.gi
    n1, n2, n3 = w_in.shape[1] // 16, w_pf.shape[1], w_pm.shape[1]
    inner = z.rows // 4

    shape = (gi, step, 128)
    row = lax.broadcasted_iota(jnp.int32, shape, 0) + (height * inner - EDGE)
    col = lax.broadcasted_iota(jnp.int32, shape, 1) + (span * (z.cols // 4) - EDGE)
    lane = lax.broadcasted_iota(jnp.int32, shape, 2)
    row_in = (row >= 0) & (row < z.heights * inner)
    wide = z.spans * (z.cols // 4)
    here = row_in & (col >= 0) & (col < wide)
    colp = col + jnp.where(lane >= n1, 1, 0)
    herep = row_in & (colp >= 0) & (colp < wide)
    mask[...] = jnp.where(here, 1.0, 0.0).reshape(z.cells, 128)
    half[...] = jnp.where(here, 0.5, 0.0).reshape(z.cells, 128)
    halfp[...] = jnp.where(herep, 0.5, 0.0).reshape(z.cells, 128)

    def masked(x, rows, ref=mask):
        m = ref[rows, :]
        return x * jnp.concatenate([m] * (x.shape[1] // 128), axis=1)

    lanes = lax.broadcasted_iota(jnp.int32, (z.strip, 128), 1)
    for copy in copies[:7]:
        copy.wait()
    for k in range(z.slots):
        q = z.planes_of(plane)[k]

        def piece(dh, ds, q=q):
            ok = (
                (q >= 0) & (q < z.planes)
                & (span + ds >= 0) & (span + ds < z.spans)
                & (height + dh >= 0) & (height + dh < z.heights)
            )
            source = (q * z.spans + span + ds) * z.heights + height + dh
            source = jnp.clip(source, 0, z.devices - 1)
            value = recv[source].astype(F32)[0 : z.strip]
            return jnp.where(ok, value, 0.0)

        tile = (noisy[0] if k == 0 else others[k - 1]).reshape(3 * z.rows, z.cols)
        ext[z.strip : z.strip + 3 * z.rows, 0 : z.cols] = tile
        for dh, base in ((-1, 0), (1, z.strip + 3 * z.rows)):
            ext[base : base + z.strip, 0 : z.cols] = piece(dh, 0).astype(BF)
            left, right = piece(dh, -1), piece(dh, 1)
            rim = jnp.where(lanes >= 128 - RIM, left, jnp.where(lanes < RIM, right, 0.0))
            ext[base : base + z.strip, z.cols : z.cols + 128] = rim.astype(BF)
        left, right = piece(0, -1), piece(0, 1)
        halves = [
            jnp.concatenate([v[0:16], v[16:32]], axis=1) for v in (left, right)
        ]
        rims = jnp.concatenate(halves, axis=0)
        rims = jnp.transpose(rims)[0 : 3 * z.rows].astype(BF)
        ext[z.strip : z.strip + 3 * z.rows, z.cols : z.cols + 128] = dot(
            rims, sides[...]
        ).astype(BF)
        patch = recv[owner[0]].astype(F32)
        patch = jnp.concatenate([patch, jnp.zeros((z.patch - z.piece, 128), F32)], axis=0)
        patch = patch.astype(BF)
        wide_rows = [dot(ext[...], across[...]).astype(BF)]
        for c in range(3):
            at = (k % 2 * 3 + c) * 128
            wide_rows.append(dot(patch, lift[at : at + 128, :]).astype(BF))
        grid[...] = dot(down[k // 2], jnp.concatenate(wide_rows, axis=0))
        for i in range(gi):
            block = grid[i * 40 : (i + 1) * 40, :]
            stack = jnp.concatenate(
                [block[:, 0:128], block[:, 128:256], block[:, 256:384], jnp.zeros((8, 128), F32)],
                axis=0,
            )
            turned = jnp.transpose(stack)
            at = i * step
            entry[at : at + step, 0:128] = turned[0:step]
            entry[at : at + step, 128:256] = turned[64 : 64 + step]
        if k == 0:
            for copy in copies[7:12]:
                copy.wait()
            b1 = bias[:, 0:n1]
            b1 = jnp.concatenate([b1] * 4, axis=1)
            b2 = bias[:, n1 : n1 + n2]
            b3 = bias[:, n1 + n2 : n1 + n2 + n3]
        per = gi
        for i in range(0, gi, per):
            rows = slice(i * step, (i + per) * step)
            x = entry[rows, :].astype(BF)
            mids = []
            for g in range(4):
                h = dot(x, w_in[:, g * 4 * n1 : (g + 1) * 4 * n1]) + b1
                h = silu(h).astype(BF)
                if k == 0:
                    h1[g, rows, :] = h
                m = silu(dot(h, w_pf[...]) + b2).astype(BF)
                if k == 0:
                    d1[rows, g * n2 : (g + 1) * n2] = m
                mids.append(m)
            low = silu(dot(jnp.concatenate(mids, axis=1), w_pm[...]) + b3).astype(BF)
            if k == 0:
                d2[rows, :] = low
            width = w_sq.shape[1]
            sq[rows, k * width : (k + 1) * width] = dot(low, w_sq[...]).astype(BF)

    def rows_of(first, last_):
        return slice(first * step // 16 * 16, up(last_ * step, 16))

    def taps(load, rows, weight, parts):
        size = up(-(-(rows.stop - rows.start) // parts), 16)
        out = []
        for first in range(rows.start, rows.stop, size):
            part = slice(first, min(first + size, rows.stop))
            out.append(dot(jnp.concatenate(load(part), axis=1), weight[...]))
        return out[0] if len(out) == 1 else jnp.concatenate(out, axis=0)

    def above(x):
        return jnp.concatenate([x[-step:], x[:-step]], axis=0)

    def below(x):
        return jnp.concatenate([x[step:], x[:step]], axis=0)

    for copy in copies[12:]:
        copy.wait()
    m = d2[...].astype(F32) + dot(sq[...], w_ac[...])
    m = masked(m, slice(0, z.cells))
    for a, ma in enumerate((above(m), m, below(m))):
        at = 3 * n3 * a
        mx[:, at + n3 : at + 2 * n3] = ma.astype(BF)
    for b, mb in enumerate((pltpu.roll(m, 1, 0), pltpu.roll(m, z.cells - 1, 0))):
        for a, ma in enumerate((above(mb), mb, below(mb))):
            at = 3 * n3 * a + 2 * b * n3
            mx[:, at : at + n3] = ma.astype(BF)

    rows = rows_of(1, gi - 1)
    n = rows.stop - rows.start
    c = silu(taps(lambda part: [mx[part, :]], rows, w_mid, 2)).astype(BF)
    v = dot(c, w_rm[...]) + d1[rows, :].astype(F32)
    v = masked(v, rows)
    for p in range(2):
        vp = v[:, 2 * p * n2 : 2 * (p + 1) * n2]
        left = pltpu.roll(vp[:, n2:], 1, 0)
        right = pltpu.roll(vp[:, :n2], n - 1, 0)
        turn = below if p == 0 else above
        for at, part in ((n2, vp), (0, left), (3 * n2, right)):
            v2[p, rows, at : at + part.shape[1]] = part.astype(BF)
            v2[3 - p, rows, at : at + part.shape[1]] = turn(part).astype(BF)

    for p in range(2):
        rows = rows_of(1, gi - 1 - p)
        n = rows.stop - rows.start
        order = ((2, 0, 1), (0, 1, 3))[p]
        e = taps(lambda part: [v2[at, part, :] for at in order], rows, w_dm, 3)
        e = silu(e).astype(BF)
        for q in range(2):
            v = dot(e[:, q * n2 : (q + 1) * n2], w_rf[...])
            v = masked(v + h1[2 * p + q, rows, :].astype(F32), rows)
            for a in range(2):
                va = v[:, 2 * a * n1 : 2 * (a + 1) * n1]
                parts = [(2 * q * n1, va)]
                if q == 0:
                    parts.append((4 * n1, pltpu.roll(va, n - 1, 0)))
                for at, part in parts:
                    v1[2 * p + a, rows, at : at + 2 * n1] = part.astype(BF)
                    if p == 0:
                        v1[4 + a, rows, at : at + 2 * n1] = below(part).astype(BF)

    for turn in range(2):
        rows = rows_of(2 - turn, gi - 2)
        n = rows.stop - rows.start
        for pair in range(2):
            lanes_in = slice(2 * pair * n1, (2 * pair + 4) * n1)
            order = ((0, 1, 2, 3), (2, 3, 4, 5))[turn]
            x = taps(lambda part: [v1[at, part, lanes_in] for at in order], rows, w_df, 3)
            for a in range(2):
                shift = step if turn and a else 0
                there = slice(rows.start + shift, rows.stop + shift)
                t = masked(
                    x[:, 2 * a * n1 : 2 * (a + 1) * n1], there, halfp if pair else half
                )
                t = t + t * jnp.tanh(t)
                parts = [((2 + 2 * pair) * n1, t)]
                if pair == 1:
                    parts.append((0, pltpu.roll(t, 1, 0)))
                for at, part in parts:
                    e1[2 * turn + a, rows, at : at + 2 * n1] = part.astype(BF)
                    if turn:
                        e1[4 + a, rows, at : at + 2 * n1] = above(part).astype(BF)

    rows = rows_of(2, gi - 2)
    outs = []
    for pair in range(2):
        lanes_in = slice(2 * pair * n1, (2 * pair + 4) * n1)
        order = (4, 5, 0, 1, 2, 3)
        outs.append(taps(lambda part: [e1[at, part, lanes_in] for at in order], rows, w_lv, 1))
    for r in range(inner):
        at = (2 + r) * step - rows.start
        block = jnp.concatenate([o[at : at + step] for o in outs], axis=0)
        last[r * 24 : (r + 1) * 24, :] = jnp.transpose(block)[0:24]
    spread_out = dot(last[...].astype(BF), spread[...]).astype(BF)
    guess = dot(gather[0], spread_out[:, 0 : z.cols])
    guess = guess + dot(gather[1], spread_out[:, z.cols :])
    pred[0] = guess.astype(BF).reshape(3, z.rows, z.cols)
    pred_copy = pltpu.make_async_copy(pred, pred_far, out_sems.at[0])
    pred_copy.start()
    given = noisy[0].reshape(3 * z.rows, z.cols).astype(F32)
    at = n1 + n2 + n3
    back, rise, keep, add = (bias[:, at + t : at + t + 1] for t in range(4))
    result = keep * ((given - back * guess) * rise) + add * guess
    sample[0] = result.reshape(3, z.rows, z.cols)
    sample_copy = pltpu.make_async_copy(sample, sample_far, out_sems.at[1])
    sample_copy.start()
    pred_copy.wait()
    sample_copy.wait()


def plan(stepnum):
    phase = (stepnum.astype(F32) / TSTEPS + 0.008) / 1.008 * (math.pi / 2.0)
    return jnp.cos(phase) ** 2


def time_bias(timestep, w_embed, w_biases):
    half = w_embed.shape[0] // 2
    freqs = jnp.exp(-math.log(10000.0) * jnp.arange(half, dtype=F32) / half)
    angles = timestep[0].astype(F32) * freqs
    waves = jnp.concatenate([jnp.sin(angles), jnp.cos(angles)])
    hidden = jax.nn.silu(jnp.dot(waves, w_embed, precision=lax.Precision.HIGHEST))
    return jnp.dot(hidden, w_biases, precision=lax.Precision.HIGHEST)


def entry_constants():
    place = np.zeros((8, 256, 128), np.float32)
    for y in range(4):
        for pair in range(2):
            for h in range(2):
                for la in range(3):
                    for lb in range(3):
                        for cin in range(6):
                            a, b = y + la, 2 * pair + h + lb
                            row = b % 2 * 128 + b // 2 * 40 + cin * 6 + a
                            place[y * 2 + pair, row, h * 64 + la * 18 + lb * 6 + cin] = 1
    return place.astype(BF)


def lay_kernel(z, count, *refs):
    far, refs = refs[:count], refs[count:]
    tile, refs = refs[0], refs[1:]
    w_in, w_pm, w_sq, w_ac, w_mid, w_rm, w_dm, w_rf, w_df, w_lv = refs[:10]
    near, refs = refs[10 : 10 + count], refs[10 + count :]
    nat, tall, leave, enter, sems = refs
    copies = fetch(tuple(zip(far, near)), sems)
    (noisy, place, w_enter, w_leave, pool_mid, w_squeeze, w_across, w_middle,
     rise_mid, decode_mid, rise_fine, decode_fine) = near
    plane = lax.axis_index("plane")
    n1, n2, n3 = decode_fine.shape[1], decode_mid.shape[1], w_middle.shape[1]

    for copy in copies:
        copy.wait()
    tile[...] = noisy[0]
    tall[...] = jnp.zeros_like(tall)
    leave[...] = jnp.zeros_like(leave)
    enter[...] = jnp.zeros_like(enter)
    blank = jnp.zeros(w_enter.shape[1:], F32)
    for a in range(3):
        leave[3 * a : 3 * a + 3, 0 : 3 * n1] = w_leave[a].astype(F32)
        for h in range(2):
            taps = w_enter[a].astype(F32)
            taps = jnp.concatenate([blank, taps] if h else [taps, blank], axis=1)
            enter[h * n1 + a * 18 : h * n1 + a * 18 + 18, :] = taps
    turned = jnp.transpose(leave[...])[0 : 3 * n1].astype(BF)
    spots = enter[...].astype(BF)
    for b in range(2):
        tall[b, b * n1 : (b + 3) * n1, :] = turned
    line = lax.broadcasted_iota(jnp.int32, (128, 128), 0)
    lane = lax.broadcasted_iota(jnp.int32, (128, 128), 1)
    for y in range(6):
        total = None
        for b in range(2):
            pick = jnp.zeros((128, 128), F32)
            for a in range(4):
                if 0 <= y - a < 3:
                    o = lane - (6 * a + 3 * b)
                    hit = (o >= 0) & (o < 3) & (line == 3 * (y - a) + o)
                    pick = jnp.where(hit, 1.0, pick)
            part = dot(tall[b], pick.astype(BF))
            total = part if total is None else total + part
        w_lv[y * 4 * n1 : (y + 1) * 4 * n1, :] = total.astype(BF)

    for y in range(4):
        for pair in range(2):
            at = ((y // 2 * 2 + pair) * 2 + y % 2) * 2 * n1
            w_in[:, at : at + 2 * n1] = dot(place[y * 2 + pair], spots).astype(BF)
    for t in range(4):
        w_pm[t * n2 : (t + 1) * n2, :] = jnp.transpose(pool_mid[t])
        w_rm[:, t * n2 : (t + 1) * n2] = jnp.transpose(rise_mid[t])
    w_sq[...] = jnp.transpose(w_squeeze[...])
    width = w_across.shape[2]
    taps = [w_across[1]]
    zero = jnp.zeros_like(taps[0])
    if z.planes == 2:
        taps.append(jnp.where(plane == 0, w_across[2], w_across[0]))
    elif z.planes > 2:
        taps.append(jnp.where(plane > 0, w_across[0], zero))
        taps.append(jnp.where(plane < z.planes - 1, w_across[2], zero))
    for k, tap in enumerate(taps):
        w_ac[k * width : (k + 1) * width, :] = jnp.transpose(tap)
    for a in range(3):
        w_mid[a * 3 * n3 : (a + 1) * 3 * n3, :] = jnp.transpose(w_middle[a])
        turned = jnp.transpose(decode_mid[a])
        at = a * 4 * n2
        w_dm[at : at + 4 * n2, :] = jnp.zeros((4 * n2, 2 * n2), BF)
        w_dm[at : at + 3 * n2, 0:n2] = turned
        w_dm[at + n2 : at + 4 * n2, n2 : 2 * n2] = turned
    w_rf[...] = jnp.transpose(rise_fine[...].reshape(4 * n1, n2))

    nat[...] = jnp.zeros_like(nat)
    for a in range(3):
        for b in range(2):
            wide = jnp.concatenate(
                [decode_fine[a].astype(F32), jnp.zeros((n1, n1), F32)], axis=1
            )
            wide = pltpu.roll(wide, b * n1, 1) if b else wide
            for r in range(2):
                nat[a + r, (2 * r + b) * n1 : (2 * r + b + 1) * n1, :] = wide.astype(BF)
    for a in range(4):
        w_df[a * 4 * n1 : (a + 1) * 4 * n1, :] = jnp.transpose(nat[a])


def solution(mesh):
    planes, spans, heights = (mesh.shape[a] for a in AXES)

    def shards(
        noisy, coarse_cond, timestep, owner, w_embed, w_biases, w_enter, pool_fine, pool_mid,
        w_squeeze, w_across, w_middle, rise_mid, decode_mid, rise_fine, decode_fine, w_leave,
    ):
        rows, cols = noisy.shape[2:]
        z = Sizes(rows, cols, planes, spans, heights, *coarse_cond.shape[3:])
        n1, n2, n3 = w_enter.shape[1], pool_fine.shape[1], pool_mid.shape[1]
        vmem = pl.BlockSpec(memory_space=pltpu.VMEM)
        smem = pl.BlockSpec(memory_space=pltpu.SMEM)
        far = pl.BlockSpec(memory_space=pltpu.HBM)
        send = pl.pallas_call(
            lambda *refs: pack_kernel(z, *refs),
            out_shape=jax.ShapeDtypeStruct((z.devices, z.piece, 128), BF),
            in_specs=[far] * 2,
            out_specs=vmem,
            scratch_shapes=[
                pltpu.VMEM(noisy.shape, BF),
                pltpu.VMEM(coarse_cond.shape, BF),
                pltpu.VMEM((planes, up(z.cond_rows, 8) + 2 * z.pad, spans * 128), F32),
                pltpu.SemaphoreType.DMA((2,)),
            ],
            compiler_params=pltpu.CompilerParams(vmem_limit_bytes=int(63.5 * 2**20)),
            name="pack",
        )(noisy, coarse_cond)
        recv = lax.all_to_all(send, AXES, 0, 0, tiled=True)
        now, prior = plan(timestep[0]), plan(timestep[0] - STRIDE)
        coefs = jnp.stack(
            [jnp.sqrt(1.0 - now), 1.0 / jnp.sqrt(now), jnp.sqrt(prior), jnp.sqrt(1.0 - prior)]
        )
        bias = jnp.concatenate([time_bias(timestep, w_embed, w_biases), coefs])[None]
        raw = (
            noisy, jnp.asarray(entry_constants()), w_enter.transpose(0, 2, 1), w_leave, pool_mid,
            w_squeeze, w_across, w_middle, rise_mid, decode_mid, rise_fine, decode_fine,
        )
        inner = w_squeeze.shape[0]
        shapes = (
            noisy.shape[1:],
            (256, 16 * n1), (4 * n2, n3), (n3, inner), (z.slots * inner, n3),
            (9 * n3, n3), (n3, 4 * n2), (12 * n2, 2 * n2), (n2, 4 * n1),
            (16 * n1, 4 * n1), (24 * n1, 128),
        )
        tile, *weights = pl.pallas_call(
            lambda *refs: lay_kernel(z, len(raw), *refs),
            out_shape=tuple(jax.ShapeDtypeStruct(shape, BF) for shape in shapes),
            in_specs=[far] * len(raw),
            out_specs=(vmem,) * len(shapes),
            scratch_shapes=[pltpu.VMEM(w.shape, BF) for w in raw]
            + [
                pltpu.VMEM((4, 4 * n1, 4 * n1), BF),
                pltpu.VMEM((2, 4 * n1, 128), BF),
                pltpu.VMEM((128, 4 * n1), F32),
                pltpu.VMEM((2 * n1, 2 * n1), F32),
                pltpu.SemaphoreType.DMA((len(raw),)),
            ],
            compiler_params=pltpu.CompilerParams(vmem_limit_bytes=int(63.5 * 2**20)),
            cost_estimate=pl.CostEstimate(
                flops=10**9, bytes_accessed=10**7, transcendentals=0
            ),
            name="lay",
        )(*raw)
        if planes == 1:
            others = tile[None]
        elif planes == 2:
            others = lax.ppermute(tile, "plane", [(0, 1), (1, 0)])[None]
        else:
            ahead = [(i, i + 1) for i in range(planes - 1)]
            behind = [(i + 1, i) for i in range(planes - 1)]
            others = jnp.stack(
                [lax.ppermute(tile, "plane", ahead), lax.ppermute(tile, "plane", behind)]
            )
        constants = [jnp.asarray(m) for m in unpack_constants(z)]
        w_pf = pool_fine.transpose(0, 2, 1).reshape(4 * n1, n2)
        operands = [
            recv, others, noisy, *constants[:4], bias, weights[0], w_pf, *weights[1:],
            *constants[4:],
        ]
        cells = z.cells
        return pl.pallas_call(
            lambda *refs: net_kernel(z, len(operands), *refs),
            out_shape=(
                jax.ShapeDtypeStruct(noisy.shape, BF),
                jax.ShapeDtypeStruct(noisy.shape, F32),
            ),
            in_specs=[smem] + [far] * len(operands),
            out_specs=(far, far),
            scratch_shapes=[pltpu.VMEM(w.shape, w.dtype) for w in operands]
            + [
                pltpu.VMEM(noisy.shape, BF),
                pltpu.VMEM(noisy.shape, F32),
                pltpu.VMEM((z.ext, cols + 128), BF),
                pltpu.VMEM((z.gi * 40, 384), F32),
                pltpu.VMEM((cells, 256), F32),
                pltpu.VMEM((4, cells, 4 * n1), BF),
                pltpu.VMEM((cells, 4 * n2), BF),
                pltpu.VMEM((cells, n3), BF),
                pltpu.VMEM((cells, z.slots * inner), BF),
                pltpu.VMEM((cells, 9 * n3), BF),
                pltpu.VMEM((4, cells, 4 * n2), BF),
                pltpu.VMEM((6, cells, 6 * n1), BF),
                pltpu.VMEM((6, cells, 6 * n1), BF),
                pltpu.VMEM((rows // 4 * 24, 2 * z.step), F32),
                pltpu.VMEM((cells, 128), F32),
                pltpu.VMEM((cells, 128), F32),
                pltpu.VMEM((cells, 128), F32),
                pltpu.SemaphoreType.DMA((len(operands),)),
                pltpu.SemaphoreType.DMA((2,)),
            ],
            compiler_params=pltpu.CompilerParams(vmem_limit_bytes=int(63.5 * 2**20)),
            name="net",
        )(owner, *operands)

    copied = P()
    in_specs = (
        P("plane", None, "height", "span"),
        P(AXES, None, None, None, None),
    ) + (copied,) * 15
    out_specs = (P("plane", None, "height", "span"), P("plane", None, "height", "span"))
    return jax.shard_map(shards, mesh=mesh, in_specs=in_specs, out_specs=out_specs, check_vma=False)
```

```python
import math

import jax
import jax.numpy as jnp
import numpy as np
from jax import lax
from jax.experimental import pallas as pl
from jax.experimental.pallas import tpu as pltpu
from jax.sharding import PartitionSpec as P

CF = 8
TSTEPS = 1000
STRIDE = 20
RIM = 9
EDGE = 2
BF = jnp.bfloat16
F32 = jnp.float32
AXES = ("plane", "span", "height")


def up(n, m):
    return -(-n // m) * m


def dot(a, b):
    return jnp.dot(a, b, preferred_element_type=F32)


def dot_nt(a, b):
    return lax.dot_general(a, b, (((1,), (1,)), ((), ())), preferred_element_type=F32)


def silu(x):
    half = 0.5 * x
    return half + half * jnp.tanh(half)


class Sizes:
    def __init__(self, rows, cols, planes, spans, heights, cond_rows, cond_cols):
        self.rows, self.cols = rows, cols
        self.planes, self.spans, self.heights = planes, spans, heights
        self.cond_rows, self.cond_cols = cond_rows, cond_cols
        self.devices = planes * spans * heights
        self.gi, self.gj = rows // 4 + 2 * EDGE, cols // 4 + 2 * EDGE
        self.step = up(self.gj, 8)
        self.cells = self.gi * self.step
        self.slots = min(planes, 3)
        self.strip = up(3 * RIM, 16)
        self.ext = 2 * self.strip + 3 * rows
        self.patch_rows, self.patch_cols = rows // CF + 4, cols // CF + 4
        self.pairs = (self.slots + 1) // 2
        self.piece = up(3 * RIM + self.patch_rows * self.pairs, 8)
        self.pad = up(3 * RIM + self.patch_rows * self.pairs, 8)
        self.patch = up(self.piece, 16)

    def planes_of(self, plane):
        if self.planes == 1:
            return [plane]
        if self.planes == 2:
            return [plane, 1 - plane]
        return [plane, plane - 1, plane + 1]


def unpack_constants(z):
    across = np.zeros((z.cols + 128, 6 * 64), np.float32)
    lift = np.zeros((2, 3, 128, 6 * 64), np.float32)
    for b in range(6):
        for j in range(z.gj):
            col = 4 * (j - EDGE) - 1 + b
            if col < 0:
                across[z.cols + 128 + col, b * 64 + j] = 1
            elif col < z.cols:
                across[col, b * 64 + j] = 1
            else:
                across[z.cols + col - z.cols, b * 64 + j] = 1
            for half in range(2):
                for c in range(3):
                    lift[half, c, half * 64 + c * z.patch_cols + col // CF + 2, b * 64 + j] = 1
    down = np.zeros((z.pairs, z.gi * 40, z.ext + 3 * z.patch), np.float32)
    for i in range(z.gi):
        for c in range(3):
            for a in range(6):
                row = 4 * (i - EDGE) - 1 + a
                if row < 0:
                    source = c * RIM + row + RIM
                elif row < z.rows:
                    source = z.strip + c * z.rows + row
                else:
                    source = z.strip + 3 * z.rows + c * RIM + row - z.rows
                down[:, i * 40 + c * 6 + a, source] = 1
                for pair in range(z.pairs):
                    at = z.ext + c * z.patch + 3 * RIM + pair * z.patch_rows + row // CF + 2
                    down[pair, i * 40 + 18 + c * 6 + a, at] = 1
    sides = np.zeros((2 * 16, 128), np.float32)
    for r in range(RIM):
        sides[r, 128 - RIM + r] = 1
        sides[16 + r, r] = 1
    spread = np.zeros((2 * z.step, 2 * z.cols), np.float32)
    for pair in range(2):
        for j in range(z.cols // 4):
            for b in range(2):
                spread[pair * z.step + j + EDGE, b * z.cols + 4 * j + 2 * pair + b] = 1
    inner = z.rows // 4
    gather = np.zeros((2, 3 * z.rows, inner * 24), np.float32)
    for b in range(2):
        for i in range(inner):
            for a in range(4):
                for o in range(3):
                    gather[b, o * z.rows + 4 * i + a, i * 24 + a * 6 + b * 3 + o] = 1
    return tuple(
        m.astype(BF) for m in (sides, across, lift.reshape(-1, 6 * 64), down, spread, gather)
    )


def fetch(pairs, sems):
    copies = [
        pltpu.make_async_copy(source, target, sems.at[n])
        for n, (source, target) in enumerate(pairs)
    ]
    for copy in copies:
        copy.start()
    return copies


def pack_kernel(z, noisy_hbm, slot_hbm, send, noisy, slot, padded, sems):
    tile_copy, slot_copy = fetch(((noisy_hbm, noisy), (slot_hbm, slot)), sems)
    plane, span, height = (lax.axis_index(a) for a in AXES)
    tall, across = z.rows // CF, z.cols // CF

    shape = (z.cond_cols, z.spans * 128)
    col = lax.broadcasted_iota(jnp.int32, shape, 0)
    lane = lax.broadcasted_iota(jnp.int32, shape, 1)
    windows = []
    for c in range(3):
        x = (lane & 127) - c * z.patch_cols
        hit = (x >= 0) & (x < z.patch_cols) & (col == (lane >> 7) * across + x - 2)
        windows.append(jnp.where(hit, 1.0, 0.0).astype(BF))
    shape = (2 * z.strip, 3 * z.rows)
    row = lax.broadcasted_iota(jnp.int32, shape, 0)
    lane = lax.broadcasted_iota(jnp.int32, shape, 1)
    strips = jnp.zeros(shape, F32)
    for half, first in ((0, z.rows - RIM), (z.strip, 0)):
        for c in range(3):
            r = row - half - c * RIM
            hit = (r >= 0) & (r < RIM) & (lane == c * z.rows + first + r)
            strips = jnp.where(hit, 1.0, strips)
    strips = strips.astype(BF)
    shape = (32, z.cols)
    row = lax.broadcasted_iota(jnp.int32, shape, 0)
    lane = lax.broadcasted_iota(jnp.int32, shape, 1)
    hit = (row < RIM) & (lane == z.cols - RIM + row)
    hit = hit | ((row >= 16) & (row < 16 + RIM) & (lane == row - 16))
    sides = jnp.where(hit, 1.0, 0.0).astype(BF)

    base = 3 * RIM
    padded[...] = jnp.zeros_like(padded)
    slot_copy.wait()
    wide = None
    for c in range(3):
        part = dot(slot[0, :, c].reshape(z.planes * z.cond_rows, z.cond_cols), windows[c])
        wide = part if wide is None else wide + part
    for p in range(z.planes):
        at = z.pad + 2
        padded[p, at : at + z.cond_rows, :] = wide[p * z.cond_rows : (p + 1) * z.cond_rows]
    tile_copy.wait()
    tile = noisy[0].reshape(3 * z.rows, z.cols)
    ends = dot(strips, tile)
    cols = dot_nt(sides, tile)

    rows = lax.broadcasted_iota(jnp.int32, (z.piece, 128), 0)
    for p in range(z.planes):
        for s in range(z.spans):
            for h in range(z.heights):
                target = (p * z.spans + s) * z.heights + h
                total = jnp.zeros((z.piece, 128), F32)
                for k0 in range(0, z.slots, 2):
                    first = base + k0 // 2 * z.patch_rows
                    mine = (rows >= first) & (rows < first + z.patch_rows)
                    both = None
                    for k in range(k0, min(k0 + 2, z.slots)):
                        q = z.planes_of(p)[k]
                        if 0 <= q < z.planes:
                            at = z.pad + tall * h - first
                            part = padded[q, at : at + z.piece, s * 128 : (s + 1) * 128]
                            part = part if k == k0 else pltpu.roll(part, 64, 1)
                            both = part if both is None else both + part
                    if both is not None:
                        total = jnp.where(mine, both, total)
                send[target] = total.astype(BF)
    rest = jnp.zeros((z.piece - z.strip, 128), F32)
    blank = jnp.zeros((16, 128 - (3 * z.rows) % 128), F32)
    side = []
    for half in (0, 16):
        part = jnp.concatenate([cols[half : half + 16], blank], axis=1)
        side.append(
            jnp.concatenate([part[:, 0:128], part[:, 128:256], rest], axis=0)
        )
    ends = [
        jnp.concatenate([ends[half : half + z.strip], rest], axis=0) for half in (0, z.strip)
    ]
    for k in range(z.slots):
        q = z.planes_of(plane)[k]
        for dh in (-1, 0, 1):
            for ds in (-1, 0, 1):
                if dh == 0 and ds == 0:
                    continue
                ok = (
                    (q >= 0) & (q < z.planes)
                    & (span + ds >= 0) & (span + ds < z.spans)
                    & (height + dh >= 0) & (height + dh < z.heights)
                )

                @pl.when(ok)
                def _(q=q, dh=dh, ds=ds):
                    target = (q * z.spans + span + ds) * z.heights + height + dh
                    if dh != 0:
                        strip = ends[0 if dh > 0 else 1]
                    else:
                        strip = side[0 if ds > 0 else 1]
                    send[target] = (send[target].astype(F32) + strip).astype(BF)


def net_kernel(
    z, count, owner, *refs
):
    far, refs = refs[:count], refs[count:]
    pred_far, sample_far, refs = refs[0], refs[1], refs[2:]
    near, refs = refs[:count], refs[count:]
    (pred, sample, ext, grid, entry, h1, d1, d2, sq, mx, v2, v1, e1, last,
     mask, half, halfp, sems, out_sems) = refs
    copies = fetch(tuple(zip(far, near)), sems)
    recv, others, noisy, sides, across, lift, down, bias = near[:8]
    w_in, w_pf, w_pm, w_sq, w_ac, w_mid, w_rm, w_dm, w_rf, w_df, w_lv, spread, gather = near[8:]
    plane, span, height = (lax.axis_index(a) for a in AXES)
    step, gi = z.step, z.gi
    n1, n2, n3 = w_in.shape[1] // 16, w_pf.shape[1], w_pm.shape[1]
    inner = z.rows // 4

    shape = (gi, step, 128)
    row = lax.broadcasted_iota(jnp.int32, shape, 0) + (height * inner - EDGE)
    col = lax.broadcasted_iota(jnp.int32, shape, 1) + (span * (z.cols // 4) - EDGE)
    lane = lax.broadcasted_iota(jnp.int32, shape, 2)
    row_in = (row >= 0) & (row < z.heights * inner)
    wide = z.spans * (z.cols // 4)
    here = row_in & (col >= 0) & (col < wide)
    colp = col + jnp.where(lane >= n1, 1, 0)
    herep = row_in & (colp >= 0) & (colp < wide)
    mask[...] = jnp.where(here, 1.0, 0.0).reshape(z.cells, 128)
    half[...] = jnp.where(here, 0.5, 0.0).reshape(z.cells, 128)
    halfp[...] = jnp.where(herep, 0.5, 0.0).reshape(z.cells, 128)

    def masked(x, rows, ref=mask):
        m = ref[rows, :]
        return x * jnp.concatenate([m] * (x.shape[1] // 128), axis=1)

    lanes = lax.broadcasted_iota(jnp.int32, (z.strip, 128), 1)
    for copy in copies[:4]:
        copy.wait()
    for k in range(z.slots):
        q = z.planes_of(plane)[k]

        def piece(dh, ds, q=q):
            ok = (
                (q >= 0) & (q < z.planes)
                & (span + ds >= 0) & (span + ds < z.spans)
                & (height + dh >= 0) & (height + dh < z.heights)
            )
            source = (q * z.spans + span + ds) * z.heights + height + dh
            source = jnp.clip(source, 0, z.devices - 1)
            value = recv[source].astype(F32)[0 : z.strip]
            return jnp.where(ok, value, 0.0)

        tile = (noisy[0] if k == 0 else others[k - 1]).reshape(3 * z.rows, z.cols)
        ext[z.strip : z.strip + 3 * z.rows, 0 : z.cols] = tile
        for dh, base in ((-1, 0), (1, z.strip + 3 * z.rows)):
            ext[base : base + z.strip, 0 : z.cols] = piece(dh, 0).astype(BF)
            left, right = piece(dh, -1), piece(dh, 1)
            rim = jnp.where(lanes >= 128 - RIM, left, jnp.where(lanes < RIM, right, 0.0))
            ext[base : base + z.strip, z.cols : z.cols + 128] = rim.astype(BF)
        left, right = piece(0, -1), piece(0, 1)
        halves = [
            jnp.concatenate([v[0:16], v[16:32]], axis=1) for v in (left, right)
        ]
        rims = jnp.concatenate(halves, axis=0)
        rims = jnp.transpose(rims)[0 : 3 * z.rows].astype(BF)
        ext[z.strip : z.strip + 3 * z.rows, z.cols : z.cols + 128] = dot(
            rims, sides[...]
        ).astype(BF)
        if k == 0:
            for copy in copies[4:7]:
                copy.wait()
        patch = recv[owner[0]].astype(F32)
        patch = jnp.concatenate([patch, jnp.zeros((z.patch - z.piece, 128), F32)], axis=0)
        patch = patch.astype(BF)
        wide_rows = [dot(ext[...], across[...]).astype(BF)]
        for c in range(3):
            at = (k % 2 * 3 + c) * 128
            wide_rows.append(dot(patch, lift[at : at + 128, :]).astype(BF))
        grid[...] = dot(down[k // 2], jnp.concatenate(wide_rows, axis=0))
        for i in range(gi):
            block = grid[i * 40 : (i + 1) * 40, :]
            stack = jnp.concatenate(
                [block[:, 0:128], block[:, 128:256], block[:, 256:384], jnp.zeros((8, 128), F32)],
                axis=0,
            )
            turned = jnp.transpose(stack)
            at = i * step
            entry[at : at + step, 0:128] = turned[0:step]
            entry[at : at + step, 128:256] = turned[64 : 64 + step]
        if k == 0:
            for copy in copies[7:12]:
                copy.wait()
            b1 = bias[:, 0:n1]
            b1 = jnp.concatenate([b1] * 4, axis=1)
            b2 = bias[:, n1 : n1 + n2]
            b3 = bias[:, n1 + n2 : n1 + n2 + n3]
        per = gi
        for i in range(0, gi, per):
            rows = slice(i * step, (i + per) * step)
            x = entry[rows, :].astype(BF)
            mids = []
            for g in range(4):
                h = dot(x, w_in[:, g * 4 * n1 : (g + 1) * 4 * n1]) + b1
                h = silu(h).astype(BF)
                if k == 0:
                    h1[g, rows, :] = h
                m = silu(dot(h, w_pf[...]) + b2).astype(BF)
                if k == 0:
                    d1[rows, g * n2 : (g + 1) * n2] = m
                mids.append(m)
            low = silu(dot(jnp.concatenate(mids, axis=1), w_pm[...]) + b3).astype(BF)
            if k == 0:
                d2[rows, :] = low
            width = w_sq.shape[1]
            sq[rows, k * width : (k + 1) * width] = dot(low, w_sq[...]).astype(BF)

    def rows_of(first, last_):
        return slice(first * step // 16 * 16, up(last_ * step, 16))

    def taps(load, rows, weight, parts):
        size = up(-(-(rows.stop - rows.start) // parts), 16)
        out = []
        for first in range(rows.start, rows.stop, size):
            part = slice(first, min(first + size, rows.stop))
            out.append(dot(jnp.concatenate(load(part), axis=1), weight[...]))
        return out[0] if len(out) == 1 else jnp.concatenate(out, axis=0)

    def above(x):
        return jnp.concatenate([x[-step:], x[:-step]], axis=0)

    def below(x):
        return jnp.concatenate([x[step:], x[:step]], axis=0)

    for copy in copies[12:]:
        copy.wait()
    m = d2[...].astype(F32) + dot(sq[...], w_ac[...])
    m = masked(m, slice(0, z.cells))
    for a, ma in enumerate((above(m), m, below(m))):
        at = 3 * n3 * a
        mx[:, at + n3 : at + 2 * n3] = ma.astype(BF)
    for b, mb in enumerate((pltpu.roll(m, 1, 0), pltpu.roll(m, z.cells - 1, 0))):
        for a, ma in enumerate((above(mb), mb, below(mb))):
            at = 3 * n3 * a + 2 * b * n3
            mx[:, at : at + n3] = ma.astype(BF)

    rows = rows_of(1, gi - 1)
    n = rows.stop - rows.start
    c = silu(taps(lambda part: [mx[part, :]], rows, w_mid, 2)).astype(BF)
    v = dot(c, w_rm[...]) + d1[rows, :].astype(F32)
    v = masked(v, rows)
    for p in range(2):
        vp = v[:, 2 * p * n2 : 2 * (p + 1) * n2]
        left = pltpu.roll(vp[:, n2:], 1, 0)
        right = pltpu.roll(vp[:, :n2], n - 1, 0)
        turn = below if p == 0 else above
        for at, part in ((n2, vp), (0, left), (3 * n2, right)):
            v2[p, rows, at : at + part.shape[1]] = part.astype(BF)
            v2[3 - p, rows, at : at + part.shape[1]] = turn(part).astype(BF)

    for p in range(2):
        rows = rows_of(1, gi - 1 - p)
        n = rows.stop - rows.start
        order = ((2, 0, 1), (0, 1, 3))[p]
        e = taps(lambda part: [v2[at, part, :] for at in order], rows, w_dm, 4)
        e = silu(e).astype(BF)
        for q in range(2):
            v = dot(e[:, q * n2 : (q + 1) * n2], w_rf[...])
            v = masked(v + h1[2 * p + q, rows, :].astype(F32), rows)
            for a in range(2):
                va = v[:, 2 * a * n1 : 2 * (a + 1) * n1]
                parts = [(2 * q * n1, va)]
                if q == 0:
                    parts.append((4 * n1, pltpu.roll(va, n - 1, 0)))
                for at, part in parts:
                    v1[2 * p + a, rows, at : at + 2 * n1] = part.astype(BF)
                    if p == 0:
                        v1[4 + a, rows, at : at + 2 * n1] = below(part).astype(BF)

    for turn in range(2):
        rows = rows_of(2 - turn, gi - 2)
        n = rows.stop - rows.start
        for pair in range(2):
            lanes_in = slice(2 * pair * n1, (2 * pair + 4) * n1)
            order = ((0, 1, 2, 3), (2, 3, 4, 5))[turn]
            x = taps(lambda part: [v1[at, part, lanes_in] for at in order], rows, w_df, 3)
            for a in range(2):
                shift = step if turn and a else 0
                there = slice(rows.start + shift, rows.stop + shift)
                t = masked(
                    x[:, 2 * a * n1 : 2 * (a + 1) * n1], there, halfp if pair else half
                )
                t = t + t * jnp.tanh(t)
                parts = [((2 + 2 * pair) * n1, t)]
                if pair == 1:
                    parts.append((0, pltpu.roll(t, 1, 0)))
                for at, part in parts:
                    e1[2 * turn + a, rows, at : at + 2 * n1] = part.astype(BF)
                    if turn:
                        e1[4 + a, rows, at : at + 2 * n1] = above(part).astype(BF)

    rows = rows_of(2, gi - 2)
    outs = []
    for pair in range(2):
        lanes_in = slice(2 * pair * n1, (2 * pair + 4) * n1)
        order = (4, 5, 0, 1, 2, 3)
        outs.append(taps(lambda part: [e1[at, part, lanes_in] for at in order], rows, w_lv, 2))
    for r in range(inner):
        at = (2 + r) * step - rows.start
        block = jnp.concatenate([o[at : at + step] for o in outs], axis=0)
        last[r * 24 : (r + 1) * 24, :] = jnp.transpose(block)[0:24]
    spread_out = dot(last[...].astype(BF), spread[...]).astype(BF)
    guess = dot(gather[0], spread_out[:, 0 : z.cols])
    guess = guess + dot(gather[1], spread_out[:, z.cols :])
    pred[0] = guess.astype(BF).reshape(3, z.rows, z.cols)
    pred_copy = pltpu.make_async_copy(pred, pred_far, out_sems.at[0])
    pred_copy.start()
    given = noisy[0].reshape(3 * z.rows, z.cols).astype(F32)
    at = n1 + n2 + n3
    back, rise, keep, add = (bias[:, at + t : at + t + 1] for t in range(4))
    result = keep * ((given - back * guess) * rise) + add * guess
    sample[0] = result.reshape(3, z.rows, z.cols)
    sample_copy = pltpu.make_async_copy(sample, sample_far, out_sems.at[1])
    sample_copy.start()
    pred_copy.wait()
    sample_copy.wait()


def plan(stepnum):
    phase = (stepnum.astype(F32) / TSTEPS + 0.008) / 1.008 * (math.pi / 2.0)
    return jnp.cos(phase) ** 2


def time_bias(timestep, w_embed, w_biases):
    half = w_embed.shape[0] // 2
    freqs = jnp.exp(-math.log(10000.0) * jnp.arange(half, dtype=F32) / half)
    angles = timestep[0].astype(F32) * freqs
    waves = jnp.concatenate([jnp.sin(angles), jnp.cos(angles)])
    hidden = jax.nn.silu(jnp.dot(waves, w_embed, precision=lax.Precision.HIGHEST))
    return jnp.dot(hidden, w_biases, precision=lax.Precision.HIGHEST)


def entry_constants():
    place = np.zeros((8, 256, 128), np.float32)
    for y in range(4):
        for pair in range(2):
            for h in range(2):
                for la in range(3):
                    for lb in range(3):
                        for cin in range(6):
                            a, b = y + la, 2 * pair + h + lb
                            row = b % 2 * 128 + b // 2 * 40 + cin * 6 + a
                            place[y * 2 + pair, row, h * 64 + la * 18 + lb * 6 + cin] = 1
    return place.astype(BF)


def lay_kernel(z, count, *refs):
    far, refs = refs[:count], refs[count:]
    tile, refs = refs[0], refs[1:]
    w_in, w_pm, w_sq, w_ac, w_mid, w_rm, w_dm, w_rf, w_df, w_lv = refs[:10]
    near, refs = refs[10 : 10 + count], refs[10 + count :]
    nat, tall, leave, enter, sems = refs
    copies = fetch(tuple(zip(far, near)), sems)
    (noisy, place, w_enter, w_leave, pool_mid, w_squeeze, w_across, w_middle,
     rise_mid, decode_mid, rise_fine, decode_fine) = near
    plane = lax.axis_index("plane")
    n1, n2, n3 = decode_fine.shape[1], decode_mid.shape[1], w_middle.shape[1]

    for copy in copies:
        copy.wait()
    tile[...] = noisy[0]
    tall[...] = jnp.zeros_like(tall)
    leave[...] = jnp.zeros_like(leave)
    enter[...] = jnp.zeros_like(enter)
    blank = jnp.zeros(w_enter.shape[1:], F32)
    for a in range(3):
        leave[3 * a : 3 * a + 3, 0 : 3 * n1] = w_leave[a].astype(F32)
        for h in range(2):
            taps = w_enter[a].astype(F32)
            taps = jnp.concatenate([blank, taps] if h else [taps, blank], axis=1)
            enter[h * n1 + a * 18 : h * n1 + a * 18 + 18, :] = taps
    turned = jnp.transpose(leave[...])[0 : 3 * n1].astype(BF)
    spots = enter[...].astype(BF)
    for b in range(2):
        tall[b, b * n1 : (b + 3) * n1, :] = turned
    line = lax.broadcasted_iota(jnp.int32, (128, 128), 0)
    lane = lax.broadcasted_iota(jnp.int32, (128, 128), 1)
    for y in range(6):
        total = None
        for b in range(2):
            pick = jnp.zeros((128, 128), F32)
            for a in range(4):
                if 0 <= y - a < 3:
                    o = lane - (6 * a + 3 * b)
                    hit = (o >= 0) & (o < 3) & (line == 3 * (y - a) + o)
                    pick = jnp.where(hit, 1.0, pick)
            part = dot(tall[b], pick.astype(BF))
            total = part if total is None else total + part
        w_lv[y * 4 * n1 : (y + 1) * 4 * n1, :] = total.astype(BF)

    for y in range(4):
        for pair in range(2):
            at = ((y // 2 * 2 + pair) * 2 + y % 2) * 2 * n1
            w_in[:, at : at + 2 * n1] = dot(place[y * 2 + pair], spots).astype(BF)
    for t in range(4):
        w_pm[t * n2 : (t + 1) * n2, :] = jnp.transpose(pool_mid[t])
        w_rm[:, t * n2 : (t + 1) * n2] = jnp.transpose(rise_mid[t])
    w_sq[...] = jnp.transpose(w_squeeze[...])
    width = w_across.shape[2]
    taps = [w_across[1]]
    zero = jnp.zeros_like(taps[0])
    if z.planes == 2:
        taps.append(jnp.where(plane == 0, w_across[2], w_across[0]))
    elif z.planes > 2:
        taps.append(jnp.where(plane > 0, w_across[0], zero))
        taps.append(jnp.where(plane < z.planes - 1, w_across[2], zero))
    for k, tap in enumerate(taps):
        w_ac[k * width : (k + 1) * width, :] = jnp.transpose(tap)
    for a in range(3):
        w_mid[a * 3 * n3 : (a + 1) * 3 * n3, :] = jnp.transpose(w_middle[a])
        turned = jnp.transpose(decode_mid[a])
        at = a * 4 * n2
        w_dm[at : at + 4 * n2, :] = jnp.zeros((4 * n2, 2 * n2), BF)
        w_dm[at : at + 3 * n2, 0:n2] = turned
        w_dm[at + n2 : at + 4 * n2, n2 : 2 * n2] = turned
    w_rf[...] = jnp.transpose(rise_fine[...].reshape(4 * n1, n2))

    nat[...] = jnp.zeros_like(nat)
    for a in range(3):
        for b in range(2):
            wide = jnp.concatenate(
                [decode_fine[a].astype(F32), jnp.zeros((n1, n1), F32)], axis=1
            )
            wide = pltpu.roll(wide, b * n1, 1) if b else wide
            for r in range(2):
                nat[a + r, (2 * r + b) * n1 : (2 * r + b + 1) * n1, :] = wide.astype(BF)
    for a in range(4):
        w_df[a * 4 * n1 : (a + 1) * 4 * n1, :] = jnp.transpose(nat[a])


def solution(mesh):
    planes, spans, heights = (mesh.shape[a] for a in AXES)

    def shards(
        noisy, coarse_cond, timestep, owner, w_embed, w_biases, w_enter, pool_fine, pool_mid,
        w_squeeze, w_across, w_middle, rise_mid, decode_mid, rise_fine, decode_fine, w_leave,
    ):
        rows, cols = noisy.shape[2:]
        z = Sizes(rows, cols, planes, spans, heights, *coarse_cond.shape[3:])
        n1, n2, n3 = w_enter.shape[1], pool_fine.shape[1], pool_mid.shape[1]
        vmem = pl.BlockSpec(memory_space=pltpu.VMEM)
        smem = pl.BlockSpec(memory_space=pltpu.SMEM)
        far = pl.BlockSpec(memory_space=pltpu.HBM)
        send = pl.pallas_call(
            lambda *refs: pack_kernel(z, *refs),
            out_shape=jax.ShapeDtypeStruct((z.devices, z.piece, 128), BF),
            in_specs=[far] * 2,
            out_specs=vmem,
            scratch_shapes=[
                pltpu.VMEM(noisy.shape, BF),
                pltpu.VMEM(coarse_cond.shape, BF),
                pltpu.VMEM((planes, up(z.cond_rows, 8) + 2 * z.pad, spans * 128), F32),
                pltpu.SemaphoreType.DMA((2,)),
            ],
            compiler_params=pltpu.CompilerParams(vmem_limit_bytes=int(63.5 * 2**20)),
            name="pack",
        )(noisy, coarse_cond)
        recv = lax.all_to_all(send, AXES, 0, 0, tiled=True)
        now, prior = plan(timestep[0]), plan(timestep[0] - STRIDE)
        coefs = jnp.stack(
            [jnp.sqrt(1.0 - now), 1.0 / jnp.sqrt(now), jnp.sqrt(prior), jnp.sqrt(1.0 - prior)]
        )
        bias = jnp.concatenate([time_bias(timestep, w_embed, w_biases), coefs])[None]
        raw = (
            noisy, jnp.asarray(entry_constants()), w_enter.transpose(0, 2, 1), w_leave, pool_mid,
            w_squeeze, w_across, w_middle, rise_mid, decode_mid, rise_fine, decode_fine,
        )
        inner = w_squeeze.shape[0]
        shapes = (
            noisy.shape[1:],
            (256, 16 * n1), (4 * n2, n3), (n3, inner), (z.slots * inner, n3),
            (9 * n3, n3), (n3, 4 * n2), (12 * n2, 2 * n2), (n2, 4 * n1),
            (16 * n1, 4 * n1), (24 * n1, 128),
        )
        tile, *weights = pl.pallas_call(
            lambda *refs: lay_kernel(z, len(raw), *refs),
            out_shape=tuple(jax.ShapeDtypeStruct(shape, BF) for shape in shapes),
            in_specs=[far] * len(raw),
            out_specs=(vmem,) * len(shapes),
            scratch_shapes=[pltpu.VMEM(w.shape, BF) for w in raw]
            + [
                pltpu.VMEM((4, 4 * n1, 4 * n1), BF),
                pltpu.VMEM((2, 4 * n1, 128), BF),
                pltpu.VMEM((128, 4 * n1), F32),
                pltpu.VMEM((2 * n1, 2 * n1), F32),
                pltpu.SemaphoreType.DMA((len(raw),)),
            ],
            compiler_params=pltpu.CompilerParams(vmem_limit_bytes=int(63.5 * 2**20)),
            cost_estimate=pl.CostEstimate(
                flops=10**9, bytes_accessed=10**7, transcendentals=0
            ),
            name="lay",
        )(*raw)
        if planes == 1:
            others = tile[None]
        elif planes == 2:
            others = lax.ppermute(tile, "plane", [(0, 1), (1, 0)])[None]
        else:
            ahead = [(i, i + 1) for i in range(planes - 1)]
            behind = [(i + 1, i) for i in range(planes - 1)]
            others = jnp.stack(
                [lax.ppermute(tile, "plane", ahead), lax.ppermute(tile, "plane", behind)]
            )
        constants = [jnp.asarray(m) for m in unpack_constants(z)]
        w_pf = pool_fine.transpose(0, 2, 1).reshape(4 * n1, n2)
        operands = [
            recv, others, noisy, *constants[:4], bias, weights[0], w_pf, *weights[1:],
            *constants[4:],
        ]
        cells = z.cells
        return pl.pallas_call(
            lambda *refs: net_kernel(z, len(operands), *refs),
            out_shape=(
                jax.ShapeDtypeStruct(noisy.shape, BF),
                jax.ShapeDtypeStruct(noisy.shape, F32),
            ),
            in_specs=[smem] + [far] * len(operands),
            out_specs=(far, far),
            scratch_shapes=[pltpu.VMEM(w.shape, w.dtype) for w in operands]
            + [
                pltpu.VMEM(noisy.shape, BF),
                pltpu.VMEM(noisy.shape, F32),
                pltpu.VMEM((z.ext, cols + 128), BF),
                pltpu.VMEM((z.gi * 40, 384), F32),
                pltpu.VMEM((cells, 256), F32),
                pltpu.VMEM((4, cells, 4 * n1), BF),
                pltpu.VMEM((cells, 4 * n2), BF),
                pltpu.VMEM((cells, n3), BF),
                pltpu.VMEM((cells, z.slots * inner), BF),
                pltpu.VMEM((cells, 9 * n3), BF),
                pltpu.VMEM((4, cells, 4 * n2), BF),
                pltpu.VMEM((6, cells, 6 * n1), BF),
                pltpu.VMEM((6, cells, 6 * n1), BF),
                pltpu.VMEM((rows // 4 * 24, 2 * z.step), F32),
                pltpu.VMEM((cells, 128), F32),
                pltpu.VMEM((cells, 128), F32),
                pltpu.VMEM((cells, 128), F32),
                pltpu.SemaphoreType.DMA((len(operands),)),
                pltpu.SemaphoreType.DMA((2,)),
            ],
            compiler_params=pltpu.CompilerParams(vmem_limit_bytes=int(63.5 * 2**20)),
            name="net",
        )(owner, *operands)

    copied = P()
    in_specs = (
        P("plane", None, "height", "span"),
        P(AXES, None, None, None, None),
    ) + (copied,) * 15
    out_specs = (P("plane", None, "height", "span"), P("plane", None, "height", "span"))
    return jax.shard_map(shards, mesh=mesh, in_specs=in_specs, out_specs=out_specs, check_vma=False)
```
